32 devices in a mesh: section: 8 (over z, core), tensor: 4 (over y, x).
Axes of the slice: x: 2, y: 2, z: 4, core: 2. Of those that a mesh axis runs over, the one named last changes fastest.
Arguments:
- layer_inputs: bfloat16 [8, 8192, 128], P('section', 'tensor'), may hold values from -160 to 160
- norm_gains: float32 [8, 8192], P('section', 'tensor'), may hold values from 0.1 to 1.9
- projection: bfloat16 [8, 8192, 2048], P('section', None, 'tensor'), may hold values from -0.125 to 0.125
- head_grads: bfloat16 [8, 128, 2048], P('section', None, 'tensor'), may hold values from -2 to 2
- top_grads: bfloat16 [8192, 128], P('tensor'), may hold values from -6 to 6
Outputs:
- input_grads: bfloat16 [8, 8192, 128], P('section', 'tensor')
- gain_grads: float32 [8, 8192], P('section', 'tensor')
The draws below stay inside these ranges and needn't reach their ends.
All inputs are finite; a program needn't handle non-finite values.
Results may differ from the reference program's by a relative error of at most 0.017.
Values may be sent and summed in bfloat16 or wider, within the bound.
No kernel may reach another device: no remote copies, remote signals or barrier semaphores. Data moves between devices by JAX's collectives and lax.ppermute only.
A program may use at most 64 MiB of HBM per device.

```python
import math
import jax
import jax.numpy as jnp
from jax import lax

D = 8192
KVW = 2048
TOK = 128
LAYERS = 8
KV_DEV = 512
N_TENSOR = 4


def draw_layer_inputs(key, part):
    first, second, third = jax.random.split(jax.random.fold_in(key, 11), 3)
    base = jnp.clip(jax.random.normal(first, (LAYERS, D, TOK), jnp.float32), -5.0, 5.0)
    rise = 3.0
    position = jnp.arange(D, dtype=jnp.float32) / max(D - 1, 1)
    feature = jnp.exp(math.log(rise) * position)[None, :, None]
    feature = feature * jnp.exp(jax.random.uniform(second, (LAYERS, D, 1), jnp.float32) * math.log(4.0))
    tokens = jnp.exp(jax.random.uniform(third, (LAYERS, 1, TOK), jnp.float32) * math.log(10.0))
    return (base * feature * tokens / 4.0).astype(jnp.bfloat16)


def shard_levels(own_key, extent, pieces, low, top_value):
    gain, own = 1.0, jax.random.fold_in(own_key, 6)
    for axis_at, parts in pieces:
        steps = jnp.exp(jax.random.uniform(jax.random.fold_in(own, axis_at), (parts,), jnp.float32, low / len(pieces), top_value / len(pieces)))
        gain = gain * jnp.repeat(steps, extent[axis_at] // parts).reshape([-1 if axis == axis_at else 1 for axis in range(len(extent))])
    return gain


def gaussian(rng, dims, scale, reach, cuts=(), held_as=jnp.bfloat16):
    loudness = shard_levels(rng, dims, cuts, -0.22, 0.18) if cuts else 1.0
    array = jax.random.normal(rng, dims, jnp.float32) * scale * loudness
    return jnp.minimum(jnp.maximum(array, -reach), reach).astype(held_as)


def setup_inputs(seed: int = 0) -> dict:
    key_of = jax.random.split(jax.random.key(seed), 6)
    return {
        "layer_inputs": draw_layer_inputs(jax.random.fold_in(key_of[5], 71), 0),
        "norm_gains": jnp.clip(1.0 + 0.18 * jax.random.normal(key_of[1], (LAYERS, D), jnp.float32), 0.1, 1.9),
        "projection": gaussian(key_of[2], (LAYERS, D, KVW), KVW ** -0.5, 0.125, ((0, 8), (2, 4))),
        "head_grads": gaussian(key_of[3], (LAYERS, TOK, KVW), 0.125, 2.0, ((0, 8), (2, 4))),
        "top_grads": gaussian(key_of[4], (D, TOK), 0.5, 6.0, ((0, 4),)),
    }


epsilon = 1e-05

def one_layer(items):
    inputs, gains, weight, grads = items
    weight_blocks = weight.reshape(D, N_TENSOR, KV_DEV).astype(jnp.float32)
    grad_blocks = grads.reshape(TOK, N_TENSOR, KV_DEV).astype(jnp.float32)
    blocks = jnp.einsum('dks,rks->kdr', weight_blocks, grad_blocks)
    rounded = lax.optimization_barrier(blocks.astype(jnp.bfloat16))
    partial_value = lax.optimization_barrier(jnp.sum(rounded.astype(jnp.float32), axis=0))
    values = inputs.astype(jnp.float32)
    scale = jnp.sqrt(lax.optimization_barrier(jnp.sum(values * values, axis=0)) / D + epsilon)
    weighted = gains[:, None] * partial_value
    inner = lax.optimization_barrier(jnp.sum(weighted * values, axis=0))
    branch = weighted / scale - values * (inner / (D * scale ** 3))
    gain_grad = lax.optimization_barrier(jnp.sum(partial_value * values / scale, axis=1))
    return (branch, gain_grad)

def reference(layer_inputs, norm_gains, projection, head_grads, top_grads):
    branches, gain_grads = lax.map(one_layer, (layer_inputs, norm_gains, projection, head_grads))
    later = jnp.cumsum(branches[::-1], axis=0)[::-1]
    input_grads = (top_grads.astype(jnp.float32)[None] + later).astype(jnp.bfloat16)
    return (input_grads, gain_grads)
```

```python
import functools

import jax
import jax.numpy as jnp
from jax import lax
from jax.experimental import pallas as pl
from jax.experimental.pallas import tpu as pltpu
from jax.sharding import PartitionSpec as P

epsilon = 1e-05
F32 = jnp.float32
BF16 = jnp.bfloat16
BOTH = ("section", "tensor")


def product_kernel(order_ref, weight_ref, grads_ref, out_ref):
    out_ref[...] = lax.dot_general(
        weight_ref[...], grads_ref[...], (((1,), (1,)), ((), ())), preferred_element_type=F32
    ).astype(out_ref.dtype)


def product(order, weight, grads, blocks):
    features, depth = weight.shape
    tokens = grads.shape[0]
    rows = features // blocks
    count = order.shape[0]
    tile = min(rows, 1024)
    steps = rows // tile
    return pl.pallas_call(
        product_kernel,
        out_shape=jax.ShapeDtypeStruct((count * rows, tokens), BF16),
        grid_spec=pltpu.PrefetchScalarGridSpec(
            num_scalar_prefetch=1,
            grid=(count, steps),
            in_specs=[
                pl.BlockSpec((tile, depth), lambda j, r, order: (order[j] * steps + r, 0)),
                pl.BlockSpec((tokens, depth), lambda j, r, order: (0, 0)),
            ],
            out_specs=pl.BlockSpec((tile, tokens), lambda j, r, order: (j * steps + r, 0)),
        ),
        cost_estimate=pl.CostEstimate(
            flops=2 * count * rows * depth * tokens,
            bytes_accessed=count * rows * (depth + tokens) * 2,
            transcendentals=0,
        ),
    )(order, weight, grads)


def masks_of(count, parity):
    masks = [1 << b for b in range(count.bit_length() - 1)]
    return masks if parity == 0 else masks[::-1]


def sigma_of(count, parity):
    masks = masks_of(count, parity)
    steps = len(masks)
    table = []
    for j in range(count):
        value = 0
        for step in range(steps):
            if j >> (steps - 1 - step) & 1:
                value ^= masks[step]
        table.append(value)
    return table


def token_sum(value):
    count = lax.axis_size("tensor")
    low = 1
    while low < count:
        group = [low] if 2 * low >= count else [low, 2 * low, 3 * low]
        parts = [lax.ppermute(value, "tensor", [(i, i ^ m) for i in range(count)]) for m in group]
        value = functools.reduce(jnp.add, parts, value)
        low *= 4
    return value


def local(features, layer_inputs, norm_gains, projection, head_grads, top_grads):
    count = lax.axis_size("tensor")
    layers = lax.axis_size("section")
    place = lax.axis_index("tensor")
    layer = lax.axis_index("section")
    core = layer % 2
    values = layer_inputs[0].astype(F32)
    gains = norm_gains[0]
    weight = projection[0]
    grads = head_grads[0]
    rows, tokens = values.shape

    sigma = jnp.where(core == 0, jnp.array(sigma_of(count, 0), jnp.int32), jnp.array(sigma_of(count, 1), jnp.int32))
    order = place ^ sigma

    def exchange(value, step):
        pairs = []
        for s in range(layers):
            mask = masks_of(count, s % 2)[step]
            pairs += [(s * count + t, s * count + (t ^ mask)) for t in range(count)]
        return lax.ppermute(value, BOTH, pairs)

    half = count // 2
    sent = product(order[half:], weight, grads, count)
    came = exchange(sent, 0)
    kept = product(order[:half], weight, grads, count)
    squares = token_sum(jnp.sum(values * values, axis=0, keepdims=True))
    steps = count.bit_length() - 1
    held = [kept]
    for step in range(1, steps):
        half //= 2
        size = half * rows
        total = sum(a[size:].astype(F32) for a in held) + came[size:].astype(F32)
        held = [a[:size] for a in held] + [came[:size]]
        came = exchange(total.astype(BF16), step)
    partial_value = sum(a.astype(F32) for a in held) + came.astype(F32)

    scale = jnp.sqrt(squares / features + epsilon)
    weighted = gains[:, None] * partial_value
    inner = token_sum(jnp.sum(weighted * values, axis=0, keepdims=True))
    branch = weighted / scale - values * (inner / (features * scale**3))
    gain_grad = jnp.sum(partial_value * values / scale, axis=1)

    part = rows // 2
    swap = [(s, s ^ 1) for s in range(layers)]

    def section(value, pairs):
        return lax.ppermute(value, "section", pairs)

    mine = lax.dynamic_slice_in_dim(branch, core * part, part, 0)
    other = lax.dynamic_slice_in_dim(branch, (1 - core) * part, part, 0)
    pair = section(other.astype(BF16), swap).astype(F32)
    chip = mine + pair
    later = jnp.zeros_like(chip)
    distance = 2
    while distance < layers:
        came = section(
            (chip + later).astype(BF16), [(s, s - distance) for s in range(distance, layers)]
        )
        later = later + came.astype(F32)
        distance *= 2
    mate = section(jnp.where(core == 1, later + mine, later).astype(BF16), swap).astype(F32)
    own = later + jnp.where(core == 0, pair, 0.0)
    tail = jnp.where(core == 0, jnp.concatenate([own, mate]), jnp.concatenate([mate, own]))
    result = (top_grads.astype(F32) + branch + tail).astype(BF16)
    return (result[None], gain_grad[None])


def solution(mesh):
    placed = (
        P("section", "tensor", None),
        P("section", "tensor"),
        P("section", None, "tensor"),
        P("section", None, "tensor"),
        P("tensor", None),
    )

    def whole(layer_inputs, norm_gains, projection, head_grads, top_grads):
        return jax.shard_map(
            functools.partial(local, layer_inputs.shape[1]),
            mesh=mesh,
            in_specs=placed,
            out_specs=(P("section", "tensor", None), P("section", "tensor")),
            check_vma=False,
        )(layer_inputs, norm_gains, projection, head_grads, top_grads)

    return whole
```

```python
import jax
import jax.numpy as jnp
from jax import lax
from jax.experimental import pallas as pl
from jax.experimental.pallas import tpu as pltpu
from jax.sharding import PartitionSpec as P

epsilon = 1e-05
F32 = jnp.float32
BF16 = jnp.bfloat16
BOTH = ("section", "tensor")
WHOLE = pl.BlockSpec(memory_space=pltpu.VMEM)
LIMIT = pltpu.CompilerParams(vmem_limit_bytes=16 << 20)


def near(value):
    return pltpu.with_memory_space_constraint(value, pltpu.VMEM)


def far(value):
    return pltpu.with_memory_space_constraint(value, pltpu.HBM)


def block_of(stream, j, count):
    bits = count.bit_length() - 1
    if stream == 1:
        return j
    out = 0
    for b in range(bits):
        out = out | (((j >> b) & 1) << (bits - 1 - b))
    return out


def mask_of(stream, step, count):
    return 1 << step if stream == 0 else count >> (step + 1)


def multiply(first_ref, second_ref, grads_ref, first_out, second_out):
    for weight, out in ((first_ref, first_out), (second_ref, second_out)):
        out[0] = lax.dot_general(
            weight[...], grads_ref[...], (((1,), (1,)), ((), ())), preferred_element_type=F32
        ).astype(out.dtype)


def keep_kernel(first_ref, second_ref, grads_ref, inputs_ref, first_out, second_out, squares_out):
    rows, tokens = inputs_ref.shape
    width = min(rows, 128)

    @pl.when(pl.program_id(0) == 0)
    def _():
        def step(i, total):
            at = pl.ds(pl.multiple_of(i * width, width), width)
            value = inputs_ref[at].astype(F32)
            return total + jnp.sum((value * value).reshape(width // 8, 8, tokens), axis=0)

        squares_out[...] = lax.fori_loop(0, rows // width, step, jnp.zeros((8, tokens), F32))

    multiply(first_ref, second_ref, grads_ref, first_out, second_out)


def product(base, weight, grads, count, extra=()):
    features, depth = weight.shape
    tokens = grads.shape[0]
    part = features // count // 2
    units = count // 2

    def rows_of(stream):
        def at(i):
            block = lax.axis_index("tensor") ^ block_of(stream, i + base, count)
            return (block * 2 + stream, 0)

        return at

    out = pltpu.VMEM((units, part, tokens), BF16)
    out_shape, out_specs = [out, out], [pl.BlockSpec((1, part, tokens), lambda i: (i, 0, 0))] * 2
    if extra:
        out_shape.append(pltpu.VMEM((8, tokens), F32))
        out_specs.append(WHOLE)
    return pl.pallas_call(
        keep_kernel if extra else multiply,
        out_shape=out_shape,
        grid=(units,),
        in_specs=[
            pl.BlockSpec((part, depth), rows_of(0)),
            pl.BlockSpec((part, depth), rows_of(1)),
            pl.BlockSpec((tokens, depth), lambda i: (0, 0)),
        ]
        + [WHOLE] * len(extra),
        out_specs=out_specs,
        compiler_params=LIMIT,
        cost_estimate=pl.CostEstimate(
            flops=4 * units * part * depth * tokens,
            bytes_accessed=4 * units * part * (depth + tokens),
            transcendentals=0,
        ),
    )(far(weight), far(weight), far(grads), *extra)


def add_kernel(*refs):
    outs = refs[-2:]
    for h, out in enumerate(outs):
        units = out.shape[0]
        parts = refs[h : len(refs) - 2 : 2]
        rows = min(out.shape[1], 64)

        def step(i, _):
            at = pl.ds(pl.multiple_of(i * rows, rows), rows)
            for u in range(units):
                total = sum(p[u + units, at].astype(F32) for p in parts)
                out[u, at] = total.astype(out.dtype)
            return 0

        lax.fori_loop(0, out.shape[1] // rows, step, 0)


def tile_of(part):
    return min(part, 128)


def wide(gains_ref, start, width, tokens):
    return jnp.broadcast_to(gains_ref[:, start : start + width], (tokens, width)).T


def sum_kernel(held, *refs):
    blocks = refs[: 2 * held]
    inputs_ref, gains_ref, squares_ref, partial_out, sums_out = refs[2 * held :]
    part, tokens = blocks[0].shape[1:]
    width = tile_of(part)
    inner = jnp.zeros((8, tokens), F32)
    for start in range(0, 2 * part, width):
        h, at = start // part, pl.ds(start % part, width)
        total = sum(b[0, at].astype(F32) for b in blocks[h::2])
        partial_out[h, at] = total
        product = total * wide(gains_ref, start, width, tokens) * inputs_ref[pl.ds(start, width)].astype(F32)
        inner = inner + jnp.sum(product.reshape(width // 8, 8, tokens), axis=0)
    sums_out[...] = jnp.concatenate([squares_ref[...], inner])


def branch_kernel(features, partial_ref, inputs_ref, gains_ref, *refs):
    sums, (branch_out, other_out, upside_out) = refs[:-3], refs[-3:]
    part, tokens = partial_ref.shape[1:]
    width = tile_of(part)
    both = jnp.sum(sum(s[...] for s in sums).reshape(2, 8, tokens), axis=1)
    upside = lax.rsqrt(both[:1] / features + epsilon)
    factor = both[1:] * (upside * upside * upside / features)
    upside_out[...] = jnp.broadcast_to(upside, upside_out.shape)
    for start in range(0, 2 * part, width):
        h, at = start // part, pl.ds(start % part, width)
        weighted = partial_ref[h, at] * wide(gains_ref, start, width, tokens)
        branch_out[h, at] = weighted * upside - inputs_ref[pl.ds(start, width)].astype(F32) * factor
    core = lax.axis_index("section") & 1
    other_out[...] = branch_out[1 - core].astype(other_out.dtype)


def pair_kernel(branch_ref, came_ref, out_ref):
    core = lax.axis_index("section") & 1
    out_ref[...] = (branch_ref[core] + came_ref[...].astype(F32)).astype(out_ref.dtype)


def later_kernel(terms_ref, later_out):
    chips, sub, tokens = terms_ref.shape
    total = jnp.zeros((sub, tokens), F32)
    for z in range(chips - 1, -1, -1):
        later_out[z] = total.astype(later_out.dtype)
        total = total + terms_ref[z].astype(F32)


def mate_kernel(later_ref, branch_ref, out_ref):
    core = lax.axis_index("section") & 1
    own = branch_ref[core] * core.astype(F32)
    out_ref[...] = (later_ref[...].astype(F32) + own).astype(out_ref.dtype)


def end_kernel(branch_ref, top_ref, later_ref, came_ref, mate_ref, out_ref):
    core = lax.axis_index("section") & 1
    half = core ^ pl.program_id(0)
    own = branch_ref[half] + top_ref[half].astype(F32)

    @pl.when(pl.program_id(0) == 0)
    def _():
        pair = came_ref[...].astype(F32) * (1 - core).astype(F32)
        out_ref[0] = (own + later_ref[...].astype(F32) + pair).astype(out_ref.dtype)

    @pl.when(pl.program_id(0) == 1)
    def _():
        out_ref[0] = (own + mate_ref[...].astype(F32)).astype(out_ref.dtype)


def call(kernel, out_shape, *arrays):
    return pl.pallas_call(
        kernel,
        out_shape=out_shape,
        in_specs=[WHOLE] * len(arrays),
        out_specs=jax.tree.map(lambda _: WHOLE, out_shape),
        compiler_params=LIMIT,
    )(*(near(a) for a in arrays))


def local(features, layer_inputs, norm_gains, projection, head_grads, top_grads):
    count = lax.axis_size("tensor")
    layers = lax.axis_size("section")
    chips = layers // 2
    weight = projection[0]
    grads = head_grads[0]
    inputs = layer_inputs[0]
    rows, tokens = inputs.shape
    part = rows // 2
    sub = part // chips
    steps = count.bit_length() - 1

    def exchange(value, mask):
        return lax.ppermute(value, "tensor", [(i, i ^ mask) for i in range(count)])

    def swap(value):
        return lax.ppermute(value, "section", [(s, s ^ 1) for s in range(layers)])

    def all_to_all(value, axis, groups):
        return lax.all_to_all(value, axis, 0, 0, tiled=True, axis_index_groups=groups)

    units = count // 2
    sent = product(units, weight, grads, count)
    came = [exchange(sent[h], mask_of(h, 0, count)) for h in range(2)]
    *kept, squares = product(0, weight, grads, count, (inputs,))

    held = [*kept, *came]
    for step in range(1, steps):
        units //= 2
        total = call(add_kernel, [pltpu.VMEM((units, part, tokens), BF16)] * 2, *held)
        held += [exchange(total[h], mask_of(h, step, count)) for h in range(2)]
    partial_value, sums = call(
        lambda *refs: sum_kernel(len(held) // 2, *refs),
        [pltpu.VMEM((2, part, tokens), F32), pltpu.VMEM((16, tokens), F32)],
        *held,
        inputs,
        norm_gains,
        squares,
    )

    sums, low = [sums], 1
    while low < count:
        group = [low] if 2 * low >= count else [low, 2 * low, 3 * low]
        total = sum(sums)
        sums = [total] + [exchange(total, m) for m in group]
        low *= 4
    half = pltpu.VMEM((part, tokens), BF16)
    branch, other, upside = call(
        lambda *refs: branch_kernel(features, *refs),
        [pltpu.VMEM((2, part, tokens), F32), half, pltpu.VMEM((8, tokens), F32)],
        partial_value,
        inputs,
        norm_gains,
        *sums,
    )

    groups = [[2 * z + c for z in range(chips)] for c in range(2)]
    pair = swap(other)
    terms = all_to_all(call(pair_kernel, half, branch, pair), "section", groups)
    later = call(
        later_kernel, pltpu.VMEM((chips, sub, tokens), BF16), terms.reshape(chips, sub, tokens)
    )
    later = all_to_all(later.reshape(part, tokens), "section", groups)
    mate = swap(call(mate_kernel, half, later, branch))
    values = inputs.reshape(2, part, tokens).astype(F32)
    gain_grad = jnp.sum(partial_value * values * upside[:1], axis=2).reshape(1, rows)
    arrays = (branch, top_grads.reshape(2, part, tokens), later, pair, mate)
    result = pl.pallas_call(
        end_kernel,
        out_shape=jax.ShapeDtypeStruct((2, part, tokens), BF16),
        grid=(2,),
        in_specs=[WHOLE] * len(arrays),
        out_specs=pl.BlockSpec(
            (1, part, tokens), lambda i: ((lax.axis_index("section") & 1) ^ i, 0, 0)
        ),
        compiler_params=LIMIT,
    )(*(near(a) for a in arrays))
    return (result.reshape(1, rows, tokens), gain_grad)


def solution(mesh):
    placed = (
        P("section", "tensor", None),
        P("section", "tensor"),
        P("section", None, "tensor"),
        P("section", None, "tensor"),
        P("tensor", None),
    )

    def whole(layer_inputs, norm_gains, projection, head_grads, top_grads):
        def part(*arrays):
            return local(layer_inputs.shape[1], *arrays)

        return jax.shard_map(
            part,
            mesh=mesh,
            in_specs=placed,
            out_specs=(P("section", "tensor", None), P("section", "tensor")),
            check_vma=False,
        )(layer_inputs, norm_gains, projection, head_grads, top_grads)

    return whole
```

```python
import jax
import jax.numpy as jnp
from jax import lax
from jax.experimental import pallas as pl
from jax.experimental.pallas import tpu as pltpu
from jax.sharding import PartitionSpec as P

epsilon = 1e-05
F32 = jnp.float32
BF16 = jnp.bfloat16
BOTH = ("section", "tensor")
WHOLE = pl.BlockSpec(memory_space=pltpu.VMEM)
LIMIT = pltpu.CompilerParams(vmem_limit_bytes=16 << 20)


def near(value):
    return pltpu.with_memory_space_constraint(value, pltpu.VMEM)


def far(value):
    return pltpu.with_memory_space_constraint(value, pltpu.HBM)


def block_of(stream, j, count):
    bits = count.bit_length() - 1
    if stream == 1:
        return j
    out = 0
    for b in range(bits):
        out = out | (((j >> b) & 1) << (bits - 1 - b))
    return out


def mask_of(stream, step, count):
    return 1 << step if stream == 0 else count >> (step + 1)


def multiply(first_ref, second_ref, grads_ref, first_out, second_out):
    for weight, out in ((first_ref, first_out), (second_ref, second_out)):
        out[0] = lax.dot_general(
            weight[...], grads_ref[...], (((1,), (1,)), ((), ())), preferred_element_type=F32
        ).astype(out.dtype)


def keep_kernel(first_ref, second_ref, grads_ref, inputs_ref, first_out, second_out, squares_out):
    rows, tokens = inputs_ref.shape
    width = min(rows, 128)

    @pl.when(pl.program_id(0) == 0)
    def _():
        def step(i, total):
            at = pl.ds(pl.multiple_of(i * width, width), width)
            value = inputs_ref[at].astype(F32)
            return total + jnp.sum((value * value).reshape(width // 8, 8, tokens), axis=0)

        squares_out[...] = lax.fori_loop(0, rows // width, step, jnp.zeros((8, tokens), F32))

    multiply(first_ref, second_ref, grads_ref, first_out, second_out)


def product(base, weight, grads, count, extra=()):
    features, depth = weight.shape
    tokens = grads.shape[0]
    part = features // count // 2
    units = count // 2

    def rows_of(stream):
        def at(i):
            block = lax.axis_index("tensor") ^ block_of(stream, i + base, count)
            return (block * 2 + stream, 0)

        return at

    out = pltpu.VMEM((units, part, tokens), BF16)
    out_shape, out_specs = [out, out], [pl.BlockSpec((1, part, tokens), lambda i: (i, 0, 0))] * 2
    if extra:
        out_shape.append(pltpu.VMEM((8, tokens), F32))
        out_specs.append(WHOLE)
    return pl.pallas_call(
        keep_kernel if extra else multiply,
        out_shape=out_shape,
        grid=(units,),
        in_specs=[
            pl.BlockSpec((part, depth), rows_of(0)),
            pl.BlockSpec((part, depth), rows_of(1)),
            pl.BlockSpec((tokens, depth), lambda i: (0, 0)),
        ]
        + [WHOLE] * len(extra),
        out_specs=out_specs,
        compiler_params=LIMIT,
        cost_estimate=pl.CostEstimate(
            flops=4 * units * part * depth * tokens,
            bytes_accessed=4 * units * part * (depth + tokens),
            transcendentals=0,
        ),
    )(far(weight), far(weight), far(grads), *extra)


def add_kernel(*refs):
    outs = refs[-2:]
    for h, out in enumerate(outs):
        units = out.shape[0]
        parts = refs[h : len(refs) - 2 : 2]
        rows = min(out.shape[1], 64)

        def step(i, _):
            at = pl.ds(pl.multiple_of(i * rows, rows), rows)
            for u in range(units):
                total = sum(p[u + units, at].astype(F32) for p in parts)
                out[u, at] = total.astype(out.dtype)
            return 0

        lax.fori_loop(0, out.shape[1] // rows, step, 0)


def tile_of(part):
    return min(part, 128)


def wide(gains_ref, start, width, tokens):
    return jnp.broadcast_to(gains_ref[:, start : start + width], (tokens, width)).T


def sum_kernel(held, *refs):
    blocks = refs[: 2 * held]
    inputs_ref, gains_ref, squares_ref, partial_out, sums_out = refs[2 * held :]
    part, tokens = blocks[0].shape[1:]
    width = tile_of(part)
    inner = jnp.zeros((8, tokens), F32)
    for start in range(0, 2 * part, width):
        h, at = start // part, pl.ds(start % part, width)
        total = sum(b[0, at].astype(F32) for b in blocks[h::2])
        partial_out[h, at] = total
        product = total * wide(gains_ref, start, width, tokens) * inputs_ref[pl.ds(start, width)].astype(F32)
        inner = inner + jnp.sum(product.reshape(width // 8, 8, tokens), axis=0)
    sums_out[...] = jnp.concatenate([squares_ref[...], inner])


def branch_kernel(features, partial_ref, inputs_ref, gains_ref, *refs):
    sums, (branch_out, other_out, upside_out) = refs[:-3], refs[-3:]
    part, tokens = partial_ref.shape[1:]
    width = tile_of(part)
    both = jnp.sum(sum(s[...] for s in sums).reshape(2, 8, tokens), axis=1)
    upside = lax.rsqrt(both[:1] / features + epsilon)
    factor = both[1:] * (upside * upside * upside / features)
    upside_out[...] = jnp.broadcast_to(upside, upside_out.shape)
    for start in range(0, 2 * part, width):
        h, at = start // part, pl.ds(start % part, width)
        weighted = partial_ref[h, at] * wide(gains_ref, start, width, tokens)
        branch_out[h, at] = weighted * upside - inputs_ref[pl.ds(start, width)].astype(F32) * factor
    core = lax.axis_index("section") & 1
    other_out[...] = branch_out[1 - core].astype(other_out.dtype)


def chip_of(distance):
    return (lax.axis_index("section") >> 1) ^ distance


def pair_kernel(branch_ref, came_ref, *outs):
    core = lax.axis_index("section") & 1
    for k, out in enumerate(outs):
        q = chip_of(k)
        out[...] = (branch_ref[core, q] + came_ref[q].astype(F32)).astype(out.dtype)


def later_kernel(*refs):
    chips = len(refs) // 2
    held = refs[-1]
    for k in range(chips):
        held[chip_of(k)] = refs[k][...].astype(F32)
    total = jnp.zeros(held.shape[1:], F32)
    for z in range(chips - 1, -1, -1):
        term = held[z]
        held[z] = total
        total = total + term
    for k in range(chips):
        out = refs[chips + k]
        out[...] = held[chip_of(k)].astype(out.dtype)


def mate_kernel(branch_ref, *refs):
    later, (later_out, mate_out) = refs[:-2], refs[-2:]
    core = lax.axis_index("section") & 1
    scale = core.astype(F32)
    for k, part in enumerate(later):
        q = chip_of(k)
        later_out[q] = part[...]
        mate_out[q] = (part[...].astype(F32) + branch_ref[core, q] * scale).astype(mate_out.dtype)


def end_kernel(branch_ref, top_ref, later_ref, came_ref, mate_ref, out_ref):
    core = lax.axis_index("section") & 1
    half = core ^ pl.program_id(0)
    own = branch_ref[half] + top_ref[half].astype(F32)

    @pl.when(pl.program_id(0) == 0)
    def _():
        pair = came_ref[...].astype(F32) * (1 - core).astype(F32)
        out_ref[0] = (own + later_ref[...].astype(F32) + pair).astype(out_ref.dtype)

    @pl.when(pl.program_id(0) == 1)
    def _():
        out_ref[0] = (own + mate_ref[...].astype(F32)).astype(out_ref.dtype)


def call(kernel, out_shape, *arrays):
    return pl.pallas_call(
        kernel,
        out_shape=out_shape,
        in_specs=[WHOLE] * len(arrays),
        out_specs=jax.tree.map(lambda _: WHOLE, out_shape),
        compiler_params=LIMIT,
    )(*(near(a) for a in arrays))


def local(features, layer_inputs, norm_gains, projection, head_grads, top_grads):
    count = lax.axis_size("tensor")
    layers = lax.axis_size("section")
    chips = layers // 2
    weight = projection[0]
    grads = head_grads[0]
    inputs = layer_inputs[0]
    rows, tokens = inputs.shape
    part = rows // 2
    sub = part // chips
    steps = count.bit_length() - 1

    def exchange(value, mask):
        return lax.ppermute(value, "tensor", [(i, i ^ mask) for i in range(count)])

    def swap(value):
        return lax.ppermute(value, "section", [(s, s ^ 1) for s in range(layers)])

    def across(value, distance):
        if not distance:
            return value
        return lax.ppermute(value, "section", [(s, s ^ (2 * distance)) for s in range(layers)])

    units = count // 2
    sent = product(units, weight, grads, count)
    came = [exchange(sent[h], mask_of(h, 0, count)) for h in range(2)]
    *kept, squares = product(0, weight, grads, count, (inputs,))

    held = [*kept, *came]
    for step in range(1, steps):
        units //= 2
        total = call(add_kernel, [pltpu.VMEM((units, part, tokens), BF16)] * 2, *held)
        held += [exchange(total[h], mask_of(h, step, count)) for h in range(2)]
    partial_value, sums = call(
        lambda *refs: sum_kernel(len(held) // 2, *refs),
        [pltpu.VMEM((2, part, tokens), F32), pltpu.VMEM((16, tokens), F32)],
        *held,
        inputs,
        norm_gains,
        squares,
    )

    sums, low = [sums], 1
    while low < count:
        group = [low] if 2 * low >= count else [low, 2 * low, 3 * low]
        total = sum(sums)
        sums = [total] + [exchange(total, m) for m in group]
        low *= 4
    half = pltpu.VMEM((part, tokens), BF16)
    branch, other, upside = call(
        lambda *refs: branch_kernel(features, *refs),
        [pltpu.VMEM((2, part, tokens), F32), half, pltpu.VMEM((8, tokens), F32)],
        partial_value,
        inputs,
        norm_gains,
        *sums,
    )

    shape = (chips, sub, tokens)
    block, whole = pltpu.VMEM((sub, tokens), BF16), pltpu.VMEM(shape, BF16)
    pair = swap(other)
    halves = branch.reshape(2, *shape)
    terms = call(pair_kernel, [block] * chips, halves, pair.reshape(shape))
    terms = [across(v, k) for k, v in enumerate(terms)]
    later = pl.pallas_call(
        later_kernel,
        out_shape=[block] * chips,
        in_specs=[WHOLE] * chips,
        out_specs=[WHOLE] * chips,
        scratch_shapes=[pltpu.VMEM(shape, F32)],
        compiler_params=LIMIT,
    )(*(near(v) for v in terms))
    later = [across(v, k) for k, v in enumerate(later)]
    later, mate = call(mate_kernel, [whole] * 2, halves, *later)
    later, mate = later.reshape(part, tokens), swap(mate.reshape(part, tokens))
    values = inputs.reshape(2, part, tokens).astype(F32)
    gain_grad = jnp.sum(partial_value * values * upside[:1], axis=2).reshape(1, rows)
    arrays = (branch, top_grads.reshape(2, part, tokens), later, pair, mate)
    result = pl.pallas_call(
        end_kernel,
        out_shape=jax.ShapeDtypeStruct((2, part, tokens), BF16),
        grid=(2,),
        in_specs=[WHOLE] * len(arrays),
        out_specs=pl.BlockSpec(
            (1, part, tokens), lambda i: ((lax.axis_index("section") & 1) ^ i, 0, 0)
        ),
        compiler_params=LIMIT,
    )(*(near(a) for a in arrays))
    return (result.reshape(1, rows, tokens), gain_grad)


def solution(mesh):
    placed = (
        P("section", "tensor", None),
        P("section", "tensor"),
        P("section", None, "tensor"),
        P("section", None, "tensor"),
        P("tensor", None),
    )

    def whole(layer_inputs, norm_gains, projection, head_grads, top_grads):
        def part(*arrays):
            return local(layer_inputs.shape[1], *arrays)

        return jax.shard_map(
            part,
            mesh=mesh,
            in_specs=placed,
            out_specs=(P("section", "tensor", None), P("section", "tensor")),
            check_vma=False,
        )(layer_inputs, norm_gains, projection, head_grads, top_grads)

    return whole
```

```python
import jax
import jax.numpy as jnp
from jax import lax
from jax.experimental import pallas as pl
from jax.experimental.pallas import tpu as pltpu
from jax.sharding import PartitionSpec as P

epsilon = 1e-05
F32 = jnp.float32
BF16 = jnp.bfloat16
PIECES = 2
WHOLE = pl.BlockSpec(memory_space=pltpu.VMEM)
LIMIT = pltpu.CompilerParams(vmem_limit_bytes=16 << 20)


def near(value):
    return pltpu.with_memory_space_constraint(value, pltpu.VMEM)


def far(value):
    return pltpu.with_memory_space_constraint(value, pltpu.HBM)


def block_of(stream, j, count):
    bits = count.bit_length() - 1
    if stream == 1:
        return j
    out = 0
    for b in range(bits):
        out = out | (((j >> b) & 1) << (bits - 1 - b))
    return out


def mask_of(stream, step, count):
    return 1 << step if stream == 0 else count >> (step + 1)


def multiply(first_ref, second_ref, grads_ref, first_out, second_out):
    for weight, out in ((first_ref, first_out), (second_ref, second_out)):
        out[0] = lax.dot_general(
            weight[...], grads_ref[...], (((1,), (1,)), ((), ())), preferred_element_type=F32
        ).astype(out.dtype)


def tile_of(part):
    return min(part, 128)


def wide(gains_ref, start, width, tokens):
    return jnp.broadcast_to(gains_ref[:, start : start + width], (tokens, width)).T


def keep_kernel(first_ref, second_ref, grads_ref, inputs_ref, first_out, second_out, squares_out):
    rows, tokens = inputs_ref.shape
    width = tile_of(rows)

    @pl.when(pl.program_id(0) == 0)
    def _():
        total = jnp.zeros((8, tokens), F32)
        for start in range(0, rows, width):
            value = inputs_ref[pl.ds(start, width)].astype(F32)
            total = total + jnp.sum((value * value).reshape(width // 8, 8, tokens), axis=0)
        squares_out[...] = total

    multiply(first_ref, second_ref, grads_ref, first_out, second_out)


def product(base, weight, grads, count, extra=(), pieces=1, piece=0):
    features, depth = weight.shape
    tokens = grads.shape[0]
    part = features // count // 2 // pieces
    units = count // 2

    def rows_of(stream):
        def at(i):
            block = lax.axis_index("tensor") ^ block_of(stream, i + base, count)
            return ((block * 2 + stream) * pieces + piece, 0)

        return at

    out = pltpu.VMEM((units, part, tokens), BF16)
    out_shape, out_specs = [out, out], [pl.BlockSpec((1, part, tokens), lambda i: (i, 0, 0))] * 2
    if extra:
        out_shape.append(pltpu.VMEM((8, tokens), F32))
        out_specs.append(WHOLE)
    return pl.pallas_call(
        keep_kernel if extra else multiply,
        out_shape=out_shape,
        grid=(units,),
        in_specs=[
            pl.BlockSpec((part, depth), rows_of(0)),
            pl.BlockSpec((part, depth), rows_of(1)),
            pl.BlockSpec((tokens, depth), lambda i: (0, 0)),
        ]
        + [WHOLE] * len(extra),
        out_specs=out_specs,
        compiler_params=LIMIT,
        cost_estimate=pl.CostEstimate(
            flops=4 * units * part * depth * tokens,
            bytes_accessed=4 * units * part * (depth + tokens),
            transcendentals=0,
        ),
    )(far(weight), far(weight), far(grads), *extra)


def terms_of(refs, pieces, stream, piece):
    kept, came = refs[stream], refs[2 + 2 * piece + stream :: 2 * pieces]
    return [(kept, piece * (kept.shape[1] // pieces))] + [(c, 0) for c in came]


def add_kernel(piece, pieces, *refs):
    outs = refs[-2:]
    for h, out in enumerate(outs):
        units, size, _ = out.shape
        width = tile_of(size)
        kept = refs[h]
        parts = [(kept, piece * size)] + [(c, 0) for c in refs[2 + h : -2 : 2]]
        for u in range(units):
            for start in range(0, size, width):
                total = sum(p[u + units, pl.ds(first + start, width)].astype(F32) for p, first in parts)
                out[u, pl.ds(start, width)] = total.astype(out.dtype)


def last_add_kernel(pieces, inputs_ref, gains_ref, *refs):
    add_kernel(0, pieces, *refs[:-2], *(out.at[:1] for out in refs[-2:]))
    rows, tokens = inputs_ref.shape
    part = rows // 2
    for h, out in enumerate(refs[-2:]):
        size = out.shape[1]
        width = tile_of(size)
        for start in range(0, size, width):
            row = (h + 1) * part - size + start
            gained = inputs_ref[pl.ds(row, width)].astype(F32) * wide(gains_ref, row, width, tokens)
            out[1, pl.ds(start, width)] = gained.astype(out.dtype)


def inner_kernel(pieces, *refs):
    held, (inputs_ref, gains_ref, squares_ref, sums_out) = refs[:-4], refs[-4:]
    gained = held[-2:]
    part = held[0].shape[1]
    tokens = inputs_ref.shape[1]
    size = part // pieces
    width = tile_of(size)
    inner = jnp.zeros((8, tokens), F32)
    for h in range(2):
        for a in range(pieces):
            parts = terms_of(held, pieces, h, a)
            for start in range(0, size, width):
                row = h * part + a * size + start
                factor = wide(gains_ref, row, width, tokens) * inputs_ref[pl.ds(row, width)].astype(F32)
                product = sum(p[0, pl.ds(first + start, width)].astype(F32) for p, first in parts) * factor
                if a == pieces - 1:
                    factor = gained[h][1, pl.ds(start, width)].astype(F32)
                    total = sum(p[1, pl.ds(first + start, width)].astype(F32) for p, first in parts)
                    product = product + total * factor
                inner = inner + jnp.sum(product.reshape(width // 8, 8, tokens), axis=0)
    sums_out[...] = jnp.concatenate([squares_ref[...], inner])


def branch_kernel(features, pieces, held, *refs):
    blocks, (inputs_ref, gains_ref, *sums) = refs[:held], refs[held:-4]
    partial_out, branch_out, other_out, upside_out = refs[-4:]
    part, tokens = partial_out.shape[1:]
    size = part // pieces
    width = tile_of(size)
    both = jnp.sum(sum(s[...] for s in sums).reshape(2, 8, tokens), axis=1)
    upside = lax.rsqrt(both[:1] / features + epsilon)
    factor = both[1:] * (upside * upside * upside / features)
    upside_out[...] = jnp.broadcast_to(upside, upside_out.shape)
    for h in range(2):
        for a in range(pieces):
            parts = terms_of(blocks, pieces, h, a)
            for start in range(0, size, width):
                at = pl.ds(a * size + start, width)
                row = h * part + a * size + start
                total = sum(p[0, pl.ds(first + start, width)].astype(F32) for p, first in parts)
                partial_out[h, at] = total
                weighted = total * wide(gains_ref, row, width, tokens)
                branch_out[h, at] = weighted * upside - inputs_ref[pl.ds(row, width)].astype(F32) * factor
    core = lax.axis_index("section") & 1
    other_out[...] = branch_out[1 - core].astype(other_out.dtype)


def chip_of(distance):
    return (lax.axis_index("section") >> 1) ^ distance


def pair_kernel(branch_ref, came_ref, *outs):
    core = lax.axis_index("section") & 1
    for k, out in enumerate(outs):
        q = chip_of(k)
        out[...] = (branch_ref[core, q] + came_ref[q].astype(F32)).astype(out.dtype)


def later_kernel(*refs):
    chips = len(refs) // 2
    held = refs[-1]
    for k in range(chips):
        held[chip_of(k)] = refs[k][...].astype(F32)
    total = jnp.zeros(held.shape[1:], F32)
    for z in range(chips - 1, -1, -1):
        term = held[z]
        held[z] = total
        total = total + term
    for k in range(chips):
        out = refs[chips + k]
        out[...] = held[chip_of(k)].astype(out.dtype)


def mate_kernel(branch_ref, *refs):
    later, (later_out, mate_out) = refs[:-2], refs[-2:]
    core = lax.axis_index("section") & 1
    scale = core.astype(F32)
    for k, part in enumerate(later):
        q = chip_of(k)
        later_out[q] = part[...]
        mate_out[q] = (part[...].astype(F32) + branch_ref[core, q] * scale).astype(mate_out.dtype)


def end_kernel(branch_ref, top_ref, later_ref, came_ref, mate_ref, out_ref):
    core = lax.axis_index("section") & 1
    half = core ^ pl.program_id(0)
    own = branch_ref[half] + top_ref[half].astype(F32)

    @pl.when(pl.program_id(0) == 0)
    def _():
        pair = came_ref[...].astype(F32) * (1 - core).astype(F32)
        out_ref[0] = (own + later_ref[...].astype(F32) + pair).astype(out_ref.dtype)

    @pl.when(pl.program_id(0) == 1)
    def _():
        out_ref[0] = (own + mate_ref[...].astype(F32)).astype(out_ref.dtype)


def call(kernel, out_shape, *arrays):
    return pl.pallas_call(
        kernel,
        out_shape=out_shape,
        in_specs=[WHOLE] * len(arrays),
        out_specs=jax.tree.map(lambda _: WHOLE, out_shape),
        compiler_params=LIMIT,
    )(*(near(a) for a in arrays))


def local(features, layer_inputs, norm_gains, projection, head_grads, top_grads):
    count = lax.axis_size("tensor")
    layers = lax.axis_size("section")
    chips = layers // 2
    weight = projection[0]
    grads = head_grads[0]
    inputs = layer_inputs[0]
    rows, tokens = inputs.shape
    part = rows // 2
    sub = part // chips
    steps = count.bit_length() - 1

    def exchange(value, mask):
        return lax.ppermute(value, "tensor", [(i, i ^ mask) for i in range(count)])

    def swap(value):
        return lax.ppermute(value, "section", [(s, s ^ 1) for s in range(layers)])

    def across(value, distance):
        if not distance:
            return value
        return lax.ppermute(value, "section", [(s, s ^ (2 * distance)) for s in range(layers)])

    units = count // 2
    sent = [product(units, weight, grads, count, (), PIECES, a) for a in range(PIECES)]
    held = [[exchange(sent[a][h], mask_of(h, 0, count)) for h in range(2)] for a in range(PIECES)]
    *kept, squares = product(0, weight, grads, count, (inputs,))

    size = part // PIECES
    for step in range(1, steps):
        units //= 2
        for a in range(PIECES):
            last = step == steps - 1 and a == 0
            outs = [pltpu.VMEM((units + last, size, tokens), BF16)] * 2
            if last:
                kernel = lambda *refs: last_add_kernel(PIECES, *refs)
                total = call(kernel, outs, inputs, norm_gains, *kept, *held[a])
            else:
                total = call(lambda *refs: add_kernel(a, PIECES, *refs), outs, *kept, *held[a])
            held[a] = held[a] + [exchange(total[h], mask_of(h, step, count)) for h in range(2)]
    arrived = [v for step in range(steps) for a in range(PIECES) for v in held[a][2 * step : 2 * step + 2]]
    sums = call(
        lambda *refs: inner_kernel(PIECES, *refs),
        pltpu.VMEM((16, tokens), F32),
        *kept,
        *arrived[:-2],
        inputs,
        norm_gains,
        squares,
    )
    sums, low = [sums], 1
    while low < count:
        group = [low] if 2 * low >= count else [low, 2 * low, 3 * low]
        total = sum(sums)
        sums = [total] + [exchange(total, m) for m in group]
        low *= 4

    half = pltpu.VMEM((part, tokens), BF16)
    full = pltpu.VMEM((2, part, tokens), F32)
    held = [*kept, *arrived]
    partial_value, branch, other, upside = call(
        lambda *refs: branch_kernel(features, PIECES, len(held), *refs),
        [full, full, half, pltpu.VMEM((8, tokens), F32)],
        *held,
        inputs,
        norm_gains,
        *sums,
    )

    shape = (chips, sub, tokens)
    block, whole = pltpu.VMEM((sub, tokens), BF16), pltpu.VMEM(shape, BF16)
    pair = swap(other)
    halves = branch.reshape(2, *shape)
    terms = call(pair_kernel, [block] * chips, halves, pair.reshape(shape))
    terms = [across(v, k) for k, v in enumerate(terms)]
    later = pl.pallas_call(
        later_kernel,
        out_shape=[block] * chips,
        in_specs=[WHOLE] * chips,
        out_specs=[WHOLE] * chips,
        scratch_shapes=[pltpu.VMEM(shape, F32)],
        compiler_params=LIMIT,
    )(*(near(v) for v in terms))
    later = [across(v, k) for k, v in enumerate(later)]
    later, mate = call(mate_kernel, [whole] * 2, halves, *later)
    later, mate = later.reshape(part, tokens), swap(mate.reshape(part, tokens))
    values = inputs.reshape(2, part, tokens).astype(F32)
    gain_grad = jnp.sum(partial_value * values * upside[:1], axis=2).reshape(1, rows)
    arrays = (branch, top_grads.reshape(2, part, tokens), later, pair, mate)
    result = pl.pallas_call(
        end_kernel,
        out_shape=jax.ShapeDtypeStruct((2, part, tokens), BF16),
        grid=(2,),
        in_specs=[WHOLE] * len(arrays),
        out_specs=pl.BlockSpec(
            (1, part, tokens), lambda i: ((lax.axis_index("section") & 1) ^ i, 0, 0)
        ),
        compiler_params=LIMIT,
    )(*(near(a) for a in arrays))
    return (result.reshape(1, rows, tokens), gain_grad)


def solution(mesh):
    placed = (
        P("section", "tensor", None),
        P("section", "tensor"),
        P("section", None, "tensor"),
        P("section", None, "tensor"),
        P("tensor", None),
    )

    def whole(layer_inputs, norm_gains, projection, head_grads, top_grads):
        def part(*arrays):
            return local(layer_inputs.shape[1], *arrays)

        return jax.shard_map(
            part,
            mesh=mesh,
            in_specs=placed,
            out_specs=(P("section", "tensor", None), P("section", "tensor")),
            check_vma=False,
        )(layer_inputs, norm_gains, projection, head_grads, top_grads)

    return whole
```

```python
import jax
import jax.numpy as jnp
from jax import lax
from jax.experimental import pallas as pl
from jax.experimental.pallas import tpu as pltpu
from jax.sharding import PartitionSpec as P

epsilon = 1e-05
F32 = jnp.float32
BF16 = jnp.bfloat16
PIECES = 2
WHOLE = pl.BlockSpec(memory_space=pltpu.VMEM)
LIMIT = pltpu.CompilerParams(vmem_limit_bytes=16 << 20)


def near(value):
    return pltpu.with_memory_space_constraint(value, pltpu.VMEM)


def far(value):
    return pltpu.with_memory_space_constraint(value, pltpu.HBM)


def block_of(stream, j, count):
    bits = count.bit_length() - 1
    if stream == 1:
        return j
    out = 0
    for b in range(bits):
        out = out | (((j >> b) & 1) << (bits - 1 - b))
    return out


def mask_of(stream, step, count):
    return 1 << step if stream == 0 else count >> (step + 1)


def multiply(first_ref, second_ref, grads_ref, first_out, second_out):
    for weight, out in ((first_ref, first_out), (second_ref, second_out)):
        out[0] = lax.dot_general(
            weight[...], grads_ref[...], (((1,), (1,)), ((), ())), preferred_element_type=F32
        ).astype(out.dtype)


def tile_of(part):
    return min(part, 128)


def wide(gains_ref, start, width, tokens):
    return jnp.broadcast_to(gains_ref[:, start : start + width], (tokens, width)).T


def keep_kernel(first_ref, second_ref, grads_ref, inputs_ref, first_out, second_out, squares_out):
    rows, tokens = inputs_ref.shape
    width = tile_of(rows)

    @pl.when(pl.program_id(0) == 0)
    def _():
        total = jnp.zeros((8, tokens), F32)
        for start in range(0, rows, width):
            value = inputs_ref[pl.ds(start, width)].astype(F32)
            total = total + jnp.sum((value * value).reshape(width // 8, 8, tokens), axis=0)
        squares_out[...] = total

    multiply(first_ref, second_ref, grads_ref, first_out, second_out)


def product(base, weight, grads, count, extra=(), pieces=1, piece=0):
    features, depth = weight.shape
    tokens = grads.shape[0]
    part = features // count // 2 // pieces
    units = count // 2

    def rows_of(stream):
        def at(i):
            block = lax.axis_index("tensor") ^ block_of(stream, i + base, count)
            return ((block * 2 + stream) * pieces + piece, 0)

        return at

    out = pltpu.VMEM((units, part, tokens), BF16)
    out_shape, out_specs = [out, out], [pl.BlockSpec((1, part, tokens), lambda i: (i, 0, 0))] * 2
    if extra:
        out_shape.append(pltpu.VMEM((8, tokens), F32))
        out_specs.append(WHOLE)
    return pl.pallas_call(
        keep_kernel if extra else multiply,
        out_shape=out_shape,
        grid=(units,),
        in_specs=[
            pl.BlockSpec((part, depth), rows_of(0)),
            pl.BlockSpec((part, depth), rows_of(1)),
            pl.BlockSpec((tokens, depth), lambda i: (0, 0)),
        ]
        + [WHOLE] * len(extra),
        out_specs=out_specs,
        compiler_params=LIMIT,
        cost_estimate=pl.CostEstimate(
            flops=4 * units * part * depth * tokens,
            bytes_accessed=4 * units * part * (depth + tokens),
            transcendentals=0,
        ),
    )(far(weight), far(weight), far(grads), *extra)


def terms_of(refs, pieces, stream, piece):
    kept, came = refs[stream], refs[2 + 2 * piece + stream :: 2 * pieces]
    return [(kept, piece * (kept.shape[1] // pieces))] + [(c, 0) for c in came]


def add_kernel(piece, pieces, *refs):
    outs = refs[-2:]
    for h, out in enumerate(outs):
        units, size, _ = out.shape
        width = tile_of(size)
        kept = refs[h]
        parts = [(kept, piece * size)] + [(c, 0) for c in refs[2 + h : -2 : 2]]
        for u in range(units):
            for start in range(0, size, width):
                total = sum(p[u + units, pl.ds(first + start, width)].astype(F32) for p, first in parts)
                out[u, pl.ds(start, width)] = total.astype(out.dtype)


def last_add_kernel(pieces, inputs_ref, gains_ref, *refs):
    add_kernel(0, pieces, *refs[:-2], *(out.at[:1] for out in refs[-2:]))
    rows, tokens = inputs_ref.shape
    part = rows // 2
    for h, out in enumerate(refs[-2:]):
        size = out.shape[1]
        width = tile_of(size)
        for start in range(0, size, width):
            row = (h + 1) * part - size + start
            gained = inputs_ref[pl.ds(row, width)].astype(F32) * wide(gains_ref, row, width, tokens)
            out[1, pl.ds(start, width)] = gained.astype(out.dtype)


def inner_kernel(pieces, *refs):
    held, (inputs_ref, gains_ref, squares_ref, sums_out) = refs[:-4], refs[-4:]
    gained = held[-2:]
    part = held[0].shape[1]
    tokens = inputs_ref.shape[1]
    size = part // pieces
    width = tile_of(size)
    inner = jnp.zeros((8, tokens), F32)
    for h in range(2):
        for a in range(pieces):
            parts = terms_of(held, pieces, h, a)
            for start in range(0, size, width):
                row = h * part + a * size + start
                factor = wide(gains_ref, row, width, tokens) * inputs_ref[pl.ds(row, width)].astype(F32)
                product = sum(p[0, pl.ds(first + start, width)].astype(F32) for p, first in parts) * factor
                if a == pieces - 1:
                    factor = gained[h][1, pl.ds(start, width)].astype(F32)
                    total = sum(p[1, pl.ds(first + start, width)].astype(F32) for p, first in parts)
                    product = product + total * factor
                inner = inner + jnp.sum(product.reshape(width // 8, 8, tokens), axis=0)
    sums_out[...] = jnp.concatenate([squares_ref[...], inner])


def branch_kernel(features, pieces, held, *refs):
    blocks, (inputs_ref, gains_ref, *sums) = refs[:held], refs[held:-4]
    partial_out, branch_out, other_out, upside_out = refs[-4:]
    part, tokens = partial_out.shape[1:]
    size = part // pieces
    width = tile_of(size)
    both = jnp.sum(sum(s[...] for s in sums).reshape(2, 8, tokens), axis=1)
    upside = lax.rsqrt(both[:1] / features + epsilon)
    factor = both[1:] * (upside * upside * upside / features)
    upside_out[...] = jnp.broadcast_to(upside, upside_out.shape)
    for h in range(2):
        for a in range(pieces):
            parts = terms_of(blocks, pieces, h, a)
            for start in range(0, size, width):
                at = pl.ds(a * size + start, width)
                row = h * part + a * size + start
                total = sum(p[0, pl.ds(first + start, width)].astype(F32) for p, first in parts)
                partial_out[h, at] = total
                weighted = total * wide(gains_ref, row, width, tokens)
                branch_out[h, at] = weighted * upside - inputs_ref[pl.ds(row, width)].astype(F32) * factor
    core = lax.axis_index("section") & 1
    other_out[...] = branch_out[1 - core].astype(other_out.dtype)


def chip_of(distance):
    return (lax.axis_index("section") >> 1) ^ distance


def order_of(chips):
    return sorted(range(chips), key=lambda k: (k % 2 == 0, -k))


def pair_kernel(branch_ref, came_ref, *outs):
    core = lax.axis_index("section") & 1
    for k, out in enumerate(outs):
        q = chip_of(k)
        out[...] = (branch_ref[core, q] + came_ref[q].astype(F32)).astype(out.dtype)


def later_kernel(*refs):
    chips = len(refs) // 2
    held, order = refs[-1], order_of(chips)
    for k in range(chips):
        held[chip_of(k)] = refs[order.index(k)][...].astype(F32)
    total = jnp.zeros(held.shape[1:], F32)
    for z in range(chips - 1, -1, -1):
        term = held[z]
        held[z] = total
        total = total + term
    for k in range(chips):
        out = refs[chips + k]
        out[...] = held[chip_of(k)].astype(out.dtype)


def mate_kernel(branch_ref, *refs):
    later, (later_out, mate_out) = refs[:-2], refs[-2:]
    core = lax.axis_index("section") & 1
    scale = core.astype(F32)
    for k, part in zip(order_of(len(later)), later):
        q = chip_of(k)
        later_out[q] = part[...]
        mate_out[q] = (part[...].astype(F32) + branch_ref[core, q] * scale).astype(mate_out.dtype)


def end_kernel(branch_ref, top_ref, later_ref, came_ref, mate_ref, out_ref):
    core = lax.axis_index("section") & 1
    half = core ^ pl.program_id(0)
    own = branch_ref[half] + top_ref[half].astype(F32)

    @pl.when(pl.program_id(0) == 0)
    def _():
        pair = came_ref[...].astype(F32) * (1 - core).astype(F32)
        out_ref[0] = (own + later_ref[...].astype(F32) + pair).astype(out_ref.dtype)

    @pl.when(pl.program_id(0) == 1)
    def _():
        out_ref[0] = (own + mate_ref[...].astype(F32)).astype(out_ref.dtype)


def call(kernel, out_shape, *arrays):
    return pl.pallas_call(
        kernel,
        out_shape=out_shape,
        in_specs=[WHOLE] * len(arrays),
        out_specs=jax.tree.map(lambda _: WHOLE, out_shape),
        compiler_params=LIMIT,
    )(*(near(a) for a in arrays))


def local(features, layer_inputs, norm_gains, projection, head_grads, top_grads):
    count = lax.axis_size("tensor")
    layers = lax.axis_size("section")
    chips = layers // 2
    weight = projection[0]
    grads = head_grads[0]
    inputs = layer_inputs[0]
    rows, tokens = inputs.shape
    part = rows // 2
    sub = part // chips
    steps = count.bit_length() - 1

    def exchange(value, mask):
        return lax.ppermute(value, "tensor", [(i, i ^ mask) for i in range(count)])

    def swap(value):
        return lax.ppermute(value, "section", [(s, s ^ 1) for s in range(layers)])

    def across(value, distance):
        if not distance:
            return value
        return lax.ppermute(value, "section", [(s, s ^ (2 * distance)) for s in range(layers)])

    units = count // 2
    sent = [product(units, weight, grads, count, (), PIECES, a) for a in range(PIECES)]
    held = [[exchange(sent[a][h], mask_of(h, 0, count)) for h in range(2)] for a in range(PIECES)]
    *kept, squares = product(0, weight, grads, count, (inputs,))

    size = part // PIECES
    for step in range(1, steps):
        units //= 2
        for a in range(PIECES):
            last = step == steps - 1 and a == 0
            outs = [pltpu.VMEM((units + last, size, tokens), BF16)] * 2
            if last:
                kernel = lambda *refs: last_add_kernel(PIECES, *refs)
                total = call(kernel, outs, inputs, norm_gains, *kept, *held[a])
            else:
                total = call(lambda *refs: add_kernel(a, PIECES, *refs), outs, *kept, *held[a])
            held[a] = held[a] + [exchange(total[h], mask_of(h, step, count)) for h in range(2)]
    arrived = [v for step in range(steps) for a in range(PIECES) for v in held[a][2 * step : 2 * step + 2]]
    sums = call(
        lambda *refs: inner_kernel(PIECES, *refs),
        pltpu.VMEM((16, tokens), F32),
        *kept,
        *arrived[:-2],
        inputs,
        norm_gains,
        squares,
    )
    sums, low = [sums], 1
    while low < count:
        group = [low] if 2 * low >= count else [low, 2 * low, 3 * low]
        total = sum(sums)
        sums = [total] + [exchange(total, m) for m in group]
        low *= 4

    half = pltpu.VMEM((part, tokens), BF16)
    full = pltpu.VMEM((2, part, tokens), F32)
    held = [*kept, *arrived]
    partial_value, branch, other, upside = call(
        lambda *refs: branch_kernel(features, PIECES, len(held), *refs),
        [full, full, half, pltpu.VMEM((8, tokens), F32)],
        *held,
        inputs,
        norm_gains,
        *sums,
    )

    shape = (chips, sub, tokens)
    block, whole = pltpu.VMEM((sub, tokens), BF16), pltpu.VMEM(shape, BF16)
    pair = swap(other)
    halves = branch.reshape(2, *shape)
    terms = call(pair_kernel, [block] * chips, halves, pair.reshape(shape))
    terms = [across(v, k) for k, v in enumerate(terms)]
    later = pl.pallas_call(
        later_kernel,
        out_shape=[block] * chips,
        in_specs=[WHOLE] * chips,
        out_specs=[WHOLE] * chips,
        scratch_shapes=[pltpu.VMEM(shape, F32)],
        compiler_params=LIMIT,
    )(*(near(terms[k]) for k in order_of(chips)))
    later = [across(v, k) for k, v in enumerate(later)]
    later, mate = call(mate_kernel, [whole] * 2, halves, *(later[k] for k in order_of(chips)))
    later, mate = later.reshape(part, tokens), swap(mate.reshape(part, tokens))
    values = inputs.reshape(2, part, tokens).astype(F32)
    gain_grad = jnp.sum(partial_value * values * upside[:1], axis=2).reshape(1, rows)
    arrays = (branch, top_grads.reshape(2, part, tokens), later, pair, mate)
    result = pl.pallas_call(
        end_kernel,
        out_shape=jax.ShapeDtypeStruct((2, part, tokens), BF16),
        grid=(2,),
        in_specs=[WHOLE] * len(arrays),
        out_specs=pl.BlockSpec(
            (1, part, tokens), lambda i: ((lax.axis_index("section") & 1) ^ i, 0, 0)
        ),
        compiler_params=LIMIT,
    )(*(near(a) for a in arrays))
    return (result.reshape(1, rows, tokens), gain_grad)


def solution(mesh):
    placed = (
        P("section", "tensor", None),
        P("section", "tensor"),
        P("section", None, "tensor"),
        P("section", None, "tensor"),
        P("tensor", None),
    )

    def whole(layer_inputs, norm_gains, projection, head_grads, top_grads):
        def part(*arrays):
            return local(layer_inputs.shape[1], *arrays)

        return jax.shard_map(
            part,
            mesh=mesh,
            in_specs=placed,
            out_specs=(P("section", "tensor", None), P("section", "tensor")),
            check_vma=False,
        )(layer_inputs, norm_gains, projection, head_grads, top_grads)

    return whole
```

```python
import jax
import jax.numpy as jnp
from jax import lax
from jax.experimental import pallas as pl
from jax.experimental.pallas import tpu as pltpu
from jax.sharding import PartitionSpec as P

epsilon = 1e-05
F32 = jnp.float32
BF16 = jnp.bfloat16
PIECES = 2
WHOLE = pl.BlockSpec(memory_space=pltpu.VMEM)
LIMIT = pltpu.CompilerParams(vmem_limit_bytes=16 << 20)


def near(value):
    return pltpu.with_memory_space_constraint(value, pltpu.VMEM)


def far(value):
    return pltpu.with_memory_space_constraint(value, pltpu.HBM)


def block_of(stream, j, count):
    bits = count.bit_length() - 1
    if stream == 1:
        return j
    out = 0
    for b in range(bits):
        out = out | (((j >> b) & 1) << (bits - 1 - b))
    return out


def mask_of(stream, step, count):
    return 1 << step if stream == 0 else count >> (step + 1)


def multiply(first_ref, second_ref, grads_ref, first_out, second_out):
    for weight, out in ((first_ref, first_out), (second_ref, second_out)):
        out[0] = lax.dot_general(
            weight[...], grads_ref[...], (((1,), (1,)), ((), ())), preferred_element_type=F32
        ).astype(out.dtype)


def tile_of(part):
    return min(part, 128)


def wide(gains_ref, start, width, tokens):
    return jnp.broadcast_to(gains_ref[:, start : start + width], (tokens, width)).T


def keep_kernel(first_ref, second_ref, grads_ref, inputs_ref, first_out, second_out, squares_out):
    rows, tokens = inputs_ref.shape
    width = tile_of(rows)

    @pl.when(pl.program_id(0) == 0)
    def _():
        total = jnp.zeros((8, tokens), F32)
        for start in range(0, rows, width):
            value = inputs_ref[pl.ds(start, width)].astype(F32)
            total = total + jnp.sum((value * value).reshape(width // 8, 8, tokens), axis=0)
        squares_out[...] = total

    multiply(first_ref, second_ref, grads_ref, first_out, second_out)


def product(base, weight, grads, count, extra=(), pieces=1, piece=0):
    features, depth = weight.shape
    tokens = grads.shape[0]
    part = features // count // 2 // pieces
    units = count // 2

    def rows_of(stream):
        def at(i):
            block = lax.axis_index("tensor") ^ block_of(stream, i + base, count)
            return ((block * 2 + stream) * pieces + piece, 0)

        return at

    out = pltpu.VMEM((units, part, tokens), BF16)
    out_shape, out_specs = [out, out], [pl.BlockSpec((1, part, tokens), lambda i: (i, 0, 0))] * 2
    if extra:
        out_shape.append(pltpu.VMEM((8, tokens), F32))
        out_specs.append(WHOLE)
    return pl.pallas_call(
        keep_kernel if extra else multiply,
        out_shape=out_shape,
        grid=(units,),
        in_specs=[
            pl.BlockSpec((part, depth), rows_of(0)),
            pl.BlockSpec((part, depth), rows_of(1)),
            pl.BlockSpec((tokens, depth), lambda i: (0, 0)),
        ]
        + [WHOLE] * len(extra),
        out_specs=out_specs,
        compiler_params=LIMIT,
        cost_estimate=pl.CostEstimate(
            flops=4 * units * part * depth * tokens,
            bytes_accessed=4 * units * part * (depth + tokens),
            transcendentals=0,
        ),
    )(far(weight), far(weight), far(grads), *extra)


def terms_of(refs, pieces, stream, piece):
    kept, came = refs[stream], refs[2 + 2 * piece + stream :: 2 * pieces]
    return [(kept, piece * (kept.shape[1] // pieces))] + [(c, 0) for c in came]


def add_kernel(piece, pieces, *refs):
    outs = refs[-2:]
    for h, out in enumerate(outs):
        units, size, _ = out.shape
        width = tile_of(size)
        kept = refs[h]
        parts = [(kept, piece * size)] + [(c, 0) for c in refs[2 + h : -2 : 2]]
        for u in range(units):
            for start in range(0, size, width):
                total = sum(p[u + units, pl.ds(first + start, width)].astype(F32) for p, first in parts)
                out[u, pl.ds(start, width)] = total.astype(out.dtype)


def last_add_kernel(pieces, inputs_ref, gains_ref, *refs):
    add_kernel(0, pieces, *refs[:-2], *(out.at[:1] for out in refs[-2:]))
    rows, tokens = inputs_ref.shape
    part = rows // 2
    for h, out in enumerate(refs[-2:]):
        size = out.shape[1]
        width = tile_of(size)
        for start in range(0, size, width):
            row = (h + 1) * part - size + start
            gained = inputs_ref[pl.ds(row, width)].astype(F32) * wide(gains_ref, row, width, tokens)
            out[1, pl.ds(start, width)] = gained.astype(out.dtype)


def inner_kernel(pieces, *refs):
    held, (inputs_ref, gains_ref, squares_ref, sums_out) = refs[:-4], refs[-4:]
    gained = held[-2:]
    part = held[0].shape[1]
    tokens = inputs_ref.shape[1]
    size = part // pieces
    width = tile_of(size)
    inner = jnp.zeros((8, tokens), F32)
    for h in range(2):
        for a in range(pieces):
            parts = terms_of(held, pieces, h, a)
            for start in range(0, size, width):
                row = h * part + a * size + start
                factor = wide(gains_ref, row, width, tokens) * inputs_ref[pl.ds(row, width)].astype(F32)
                product = sum(p[0, pl.ds(first + start, width)].astype(F32) for p, first in parts) * factor
                if a == pieces - 1:
                    factor = gained[h][1, pl.ds(start, width)].astype(F32)
                    total = sum(p[1, pl.ds(first + start, width)].astype(F32) for p, first in parts)
                    product = product + total * factor
                inner = inner + jnp.sum(product.reshape(width // 8, 8, tokens), axis=0)
    sums_out[...] = jnp.concatenate([squares_ref[...], inner])


def weigh_kernel(pieces, held, *refs):
    blocks, (gains_ref, partial_out, weighted_out) = refs[:held], refs[held:]
    part, tokens = partial_out.shape[1:]
    size = part // pieces
    width = tile_of(size)
    for h in range(2):
        for a in range(pieces):
            parts = terms_of(blocks, pieces, h, a)
            for start in range(0, size, width):
                at = pl.ds(a * size + start, width)
                row = h * part + a * size + start
                total = sum(p[0, pl.ds(first + start, width)].astype(F32) for p, first in parts)
                partial_out[h, at] = total
                weighted_out[h, at] = total * wide(gains_ref, row, width, tokens)


def branch_kernel(features, weighted_ref, inputs_ref, *refs):
    sums, (branch_out, other_out, upside_out) = refs[:-3], refs[-3:]
    _, part, tokens = branch_out.shape
    width = tile_of(part)
    both = jnp.sum(sum(s[...] for s in sums).reshape(2, 8, tokens), axis=1)
    upside = lax.rsqrt(both[:1] / features + epsilon)
    factor = both[1:] * (upside * upside * upside / features)
    upside_out[...] = jnp.broadcast_to(upside, upside_out.shape)
    for start in range(0, 2 * part, width):
        h, at = start // part, pl.ds(start % part, width)
        value = inputs_ref[pl.ds(start, width)].astype(F32)
        branch_out[h, at] = weighted_ref[h, at] * upside - value * factor
    core = lax.axis_index("section") & 1
    other_out[...] = branch_out[1 - core].astype(other_out.dtype)


def chip_of(distance):
    return (lax.axis_index("section") >> 1) ^ distance


def order_of(chips):
    return sorted(range(chips), key=lambda k: (k % 2 == 0, -k))


def pair_kernel(branch_ref, came_ref, *outs):
    core = lax.axis_index("section") & 1
    for k, out in enumerate(outs):
        q = chip_of(k)
        out[...] = (branch_ref[core, q] + came_ref[q].astype(F32)).astype(out.dtype)


def gain_grad_kernel(partial_ref, inputs_ref, upside_ref, out_ref, done_ref):
    done_ref[...] = upside_ref[...]
    _, part, tokens = partial_ref.shape
    width = tile_of(part)
    for start in range(0, 2 * part, width):
        product = partial_ref[start // part, pl.ds(start % part, width)] * upside_ref[:1]
        product = product * inputs_ref[pl.ds(start, width)].astype(F32)
        out_ref[:, start : start + width] = jnp.sum(product.T, axis=0, keepdims=True)


def later_kernel(*refs):
    chips = len(refs) // 2 - 1
    held, order = refs[-1], order_of(chips)
    for k in range(chips):
        held[chip_of(k)] = refs[order.index(k)][...].astype(F32)
    total = jnp.zeros(held.shape[1:], F32)
    for z in range(chips - 1, -1, -1):
        term = held[z]
        held[z] = total
        total = total + term
    for k in range(chips):
        out = refs[chips + 1 + k]
        out[...] = held[chip_of(k)].astype(out.dtype)


def mate_kernel(branch_ref, *refs):
    later, (later_out, mate_out) = refs[:-2], refs[-2:]
    core = lax.axis_index("section") & 1
    scale = core.astype(F32)
    for k, part in zip(order_of(len(later)), later):
        q = chip_of(k)
        later_out[q] = part[...]
        mate_out[q] = (part[...].astype(F32) + branch_ref[core, q] * scale).astype(mate_out.dtype)


def first_end_kernel(branch_ref, top_ref, later_ref, came_ref, out_ref):
    core = lax.axis_index("section") & 1
    pair = came_ref[...].astype(F32) * (1 - core).astype(F32)
    total = branch_ref[core] + top_ref[core].astype(F32) + later_ref[...].astype(F32) + pair
    out_ref[0] = total.astype(out_ref.dtype)


def second_end_kernel(branch_ref, top_ref, mate_ref, result_ref, out_ref):
    del result_ref
    other = 1 - (lax.axis_index("section") & 1)
    total = branch_ref[other] + top_ref[other].astype(F32) + mate_ref[...].astype(F32)
    out_ref[0] = total.astype(out_ref.dtype)


def call(kernel, out_shape, *arrays, cost=None):
    return pl.pallas_call(
        kernel,
        out_shape=out_shape,
        in_specs=[WHOLE] * len(arrays),
        out_specs=jax.tree.map(lambda _: WHOLE, out_shape),
        compiler_params=LIMIT,
        cost_estimate=cost,
    )(*(near(a) for a in arrays))


def local(features, layer_inputs, norm_gains, projection, head_grads, top_grads):
    count = lax.axis_size("tensor")
    layers = lax.axis_size("section")
    chips = layers // 2
    weight = projection[0]
    grads = head_grads[0]
    inputs = layer_inputs[0]
    rows, tokens = inputs.shape
    part = rows // 2
    sub = part // chips
    steps = count.bit_length() - 1

    def exchange(value, mask):
        return lax.ppermute(value, "tensor", [(i, i ^ mask) for i in range(count)])

    def swap(value):
        return lax.ppermute(value, "section", [(s, s ^ 1) for s in range(layers)])

    def across(value, distance):
        if not distance:
            return value
        return lax.ppermute(value, "section", [(s, s ^ (2 * distance)) for s in range(layers)])

    units = count // 2
    sent = [product(units, weight, grads, count, (), PIECES, a) for a in range(PIECES)]
    held = [[exchange(sent[a][h], mask_of(h, 0, count)) for h in range(2)] for a in range(PIECES)]
    *kept, squares = product(0, weight, grads, count, (inputs,))

    size = part // PIECES
    for step in range(1, steps):
        units //= 2
        for a in range(PIECES):
            last = step == steps - 1 and a == 0
            outs = [pltpu.VMEM((units + last, size, tokens), BF16)] * 2
            if last:
                kernel = lambda *refs: last_add_kernel(PIECES, *refs)
                total = call(kernel, outs, inputs, norm_gains, *kept, *held[a])
            else:
                total = call(lambda *refs: add_kernel(a, PIECES, *refs), outs, *kept, *held[a])
            held[a] = held[a] + [exchange(total[h], mask_of(h, step, count)) for h in range(2)]
    arrived = [v for step in range(steps) for a in range(PIECES) for v in held[a][2 * step : 2 * step + 2]]
    sums = call(
        lambda *refs: inner_kernel(PIECES, *refs),
        pltpu.VMEM((16, tokens), F32),
        *kept,
        *arrived[:-2],
        inputs,
        norm_gains,
        squares,
    )
    sums, low = [sums], 1
    while low < count:
        group = [low] if 2 * low >= count else [3 * low, 2 * low, low]
        total = sum(sums)
        sums = [total] + [exchange(total, m) for m in group]
        low *= 4

    half = pltpu.VMEM((part, tokens), BF16)
    full = pltpu.VMEM((2, part, tokens), F32)
    held = [*kept, *arrived]
    partial_value, weighted = call(
        lambda *refs: weigh_kernel(PIECES, len(held), *refs),
        [full, full],
        *held,
        norm_gains,
        cost=pl.CostEstimate(flops=1 << 32, bytes_accessed=1 << 20, transcendentals=0),
    )
    branch, other, upside = call(
        lambda *refs: branch_kernel(features, *refs),
        [full, half, pltpu.VMEM((8, tokens), F32)],
        weighted,
        inputs,
        *sums,
    )

    shape = (chips, sub, tokens)
    block, whole = pltpu.VMEM((sub, tokens), BF16), pltpu.VMEM(shape, BF16)
    pair = swap(other)
    halves = branch.reshape(2, *shape)
    terms = call(pair_kernel, [block] * chips, halves, pair.reshape(shape))
    terms = [across(v, k) for k, v in enumerate(terms)]
    gain_grad, done = call(
        gain_grad_kernel,
        [jax.ShapeDtypeStruct((1, rows), F32), pltpu.VMEM((8, tokens), F32)],
        partial_value,
        inputs,
        upside,
    )
    later = pl.pallas_call(
        later_kernel,
        out_shape=[block] * chips,
        in_specs=[WHOLE] * chips + [pl.BlockSpec(memory_space=pl.ANY)],
        out_specs=[WHOLE] * chips,
        scratch_shapes=[pltpu.VMEM(shape, F32)],
        compiler_params=LIMIT,
    )(*(near(terms[k]) for k in order_of(chips)), done)
    later = [across(v, k) for k, v in enumerate(later)]
    later, mate = call(mate_kernel, [whole] * 2, halves, *(later[k] for k in order_of(chips)))
    later, mate = later.reshape(part, tokens), swap(mate.reshape(part, tokens))
    top = near(top_grads.reshape(2, part, tokens))

    def end(kernel, half, arrays, into):
        return pl.pallas_call(
            kernel,
            out_shape=jax.ShapeDtypeStruct((2, part, tokens), BF16),
            grid=(1,),
            in_specs=[WHOLE] * len(arrays) + [pl.BlockSpec(memory_space=pl.ANY)] * len(into),
            out_specs=pl.BlockSpec((1, part, tokens), lambda i: (half(lax.axis_index("section") & 1), 0, 0)),
            input_output_aliases={len(arrays): 0} if into else {},
            compiler_params=LIMIT,
        )(*(near(a) for a in arrays), *into)

    result = end(first_end_kernel, lambda core: core, (branch, top, later, pair), ())
    result = end(second_end_kernel, lambda core: 1 - core, (branch, top, mate), (result,))
    return (result.reshape(1, rows, tokens), gain_grad)


def solution(mesh):
    placed = (
        P("section", "tensor", None),
        P("section", "tensor"),
        P("section", None, "tensor"),
        P("section", None, "tensor"),
        P("tensor", None),
    )

    def whole(layer_inputs, norm_gains, projection, head_grads, top_grads):
        def part(*arrays):
            return local(layer_inputs.shape[1], *arrays)

        return jax.shard_map(
            part,
            mesh=mesh,
            in_specs=placed,
            out_specs=(P("section", "tensor", None), P("section", "tensor")),
            check_vma=False,
        )(layer_inputs, norm_gains, projection, head_grads, top_grads)

    return whole
```

```python
import jax
import jax.numpy as jnp
from jax import lax
from jax.experimental import pallas as pl
from jax.experimental.pallas import tpu as pltpu
from jax.sharding import PartitionSpec as P

epsilon = 1e-05
F32 = jnp.float32
BF16 = jnp.bfloat16
PIECES = 2
WHOLE = pl.BlockSpec(memory_space=pltpu.VMEM)
LIMIT = pltpu.CompilerParams(vmem_limit_bytes=16 << 20)


def near(value):
    return pltpu.with_memory_space_constraint(value, pltpu.VMEM)


def far(value):
    return pltpu.with_memory_space_constraint(value, pltpu.HBM)


def block_of(stream, j, count):
    bits = count.bit_length() - 1
    if stream == 1:
        return j
    out = 0
    for b in range(bits):
        out = out | (((j >> b) & 1) << (bits - 1 - b))
    return out


def mask_of(stream, step, count):
    return 1 << step if stream == 0 else count >> (step + 1)


def multiply(first_ref, second_ref, grads_ref, first_out, second_out):
    for weight, out in ((first_ref, first_out), (second_ref, second_out)):
        out[0] = lax.dot_general(
            weight[...], grads_ref[...], (((1,), (1,)), ((), ())), preferred_element_type=F32
        ).astype(out.dtype)


def tile_of(part):
    return min(part, 128)


def wide(gains_ref, start, width, tokens):
    return jnp.broadcast_to(gains_ref[:, start : start + width], (tokens, width)).T


def keep_kernel(first_ref, second_ref, grads_ref, inputs_ref, first_out, second_out, squares_out):
    rows, tokens = inputs_ref.shape
    width = tile_of(rows)

    @pl.when(pl.program_id(0) == 0)
    def _():
        total = jnp.zeros((8, tokens), F32)
        for start in range(0, rows, width):
            value = inputs_ref[pl.ds(start, width)].astype(F32)
            total = total + jnp.sum((value * value).reshape(width // 8, 8, tokens), axis=0)
        squares_out[...] = total

    multiply(first_ref, second_ref, grads_ref, first_out, second_out)


def product(base, weight, grads, count, extra=(), pieces=1, piece=0):
    features, depth = weight.shape
    tokens = grads.shape[0]
    part = features // count // 2 // pieces
    units = count // 2

    def rows_of(stream):
        def at(i):
            block = lax.axis_index("tensor") ^ block_of(stream, i + base, count)
            return ((block * 2 + stream) * pieces + piece, 0)

        return at

    out = pltpu.VMEM((units, part, tokens), BF16)
    out_shape, out_specs = [out, out], [pl.BlockSpec((1, part, tokens), lambda i: (i, 0, 0))] * 2
    if extra:
        out_shape.append(pltpu.VMEM((8, tokens), F32))
        out_specs.append(WHOLE)
    return pl.pallas_call(
        keep_kernel if extra else multiply,
        out_shape=out_shape,
        grid=(units,),
        in_specs=[
            pl.BlockSpec((part, depth), rows_of(0)),
            pl.BlockSpec((part, depth), rows_of(1)),
            pl.BlockSpec((tokens, depth), lambda i: (0, 0)),
        ]
        + [WHOLE] * len(extra),
        out_specs=out_specs,
        compiler_params=LIMIT,
        cost_estimate=pl.CostEstimate(
            flops=4 * units * part * depth * tokens,
            bytes_accessed=4 * units * part * (depth + tokens),
            transcendentals=0,
        ),
    )(far(weight), far(weight), far(grads), *extra)


def terms_of(refs, pieces, stream, piece):
    kept, came = refs[stream], refs[2 + 2 * piece + stream :: 2 * pieces]
    return [(kept, piece * (kept.shape[1] // pieces))] + [(c, 0) for c in came]


def add_kernel(piece, pieces, *refs):
    outs = refs[-2:]
    for h, out in enumerate(outs):
        units, size, _ = out.shape
        width = tile_of(size)
        kept = refs[h]
        parts = [(kept, piece * size)] + [(c, 0) for c in refs[2 + h : -2 : 2]]
        for u in range(units):
            for start in range(0, size, width):
                total = sum(p[u + units, pl.ds(first + start, width)].astype(F32) for p, first in parts)
                out[u, pl.ds(start, width)] = total.astype(out.dtype)


def last_add_kernel(pieces, inputs_ref, gains_ref, *refs):
    add_kernel(0, pieces, *refs[:-2], *(out.at[:1] for out in refs[-2:]))
    rows, tokens = inputs_ref.shape
    part = rows // 2
    for h, out in enumerate(refs[-2:]):
        size = out.shape[1]
        width = tile_of(size)
        for start in range(0, size, width):
            row = (h + 1) * part - size + start
            gained = inputs_ref[pl.ds(row, width)].astype(F32) * wide(gains_ref, row, width, tokens)
            out[1, pl.ds(start, width)] = gained.astype(out.dtype)


def early_kernel(pieces, *refs):
    held, (inputs_ref, gains_ref, inner_out, pairs_out, gained_out) = refs[:-5], refs[-5:]
    part = held[0].shape[1]
    tokens = inputs_ref.shape[1]
    size = part // pieces
    width = tile_of(size)
    inner = jnp.zeros((8, tokens), F32)
    for h in range(2):
        for a in range(pieces):
            parts = terms_of(held, pieces, h, a)
            for start in range(0, size, width):
                row = h * part + a * size + start
                factor = wide(gains_ref, row, width, tokens) * inputs_ref[pl.ds(row, width)].astype(F32)
                product = sum(p[0, pl.ds(first + start, width)].astype(F32) for p, first in parts) * factor
                inner = inner + jnp.sum(product.reshape(width // 8, 8, tokens), axis=0)
                if a == pieces - 1:
                    total = sum(p[1, pl.ds(first + start, width)].astype(F32) for p, first in parts)
                    pairs_out[h, pl.ds(start, width)] = total
                else:
                    gained_out[h, pl.ds(a * size + start, width)] = factor
    inner_out[...] = inner


def inner_kernel(pieces, inner_ref, pairs_ref, gained_ref, squares_ref, *refs):
    came, sums_out = refs[:-1], refs[-1]
    _, size, tokens = pairs_ref.shape
    width = tile_of(size)
    inner = inner_ref[...]
    for h in range(2):
        for start in range(0, size, width):
            at = pl.ds(start, width)
            product = pairs_ref[h, at] * came[h][1, at].astype(F32)
            for a in range(pieces - 1):
                product = product + gained_ref[h, pl.ds(a * size + start, width)] * came[2 * a + h][0, at].astype(F32)
            inner = inner + jnp.sum(product.reshape(width // 8, 8, tokens), axis=0)
    sums_out[...] = jnp.concatenate([squares_ref[...], inner])


def weigh_kernel(pieces, held, *refs):
    blocks, (gains_ref, partial_out, weighted_out) = refs[:held], refs[held:]
    part, tokens = partial_out.shape[1:]
    size = part // pieces
    width = tile_of(size)
    for h in range(2):
        for a in range(pieces):
            parts = terms_of(blocks, pieces, h, a)
            for start in range(0, size, width):
                at = pl.ds(a * size + start, width)
                row = h * part + a * size + start
                total = sum(p[0, pl.ds(first + start, width)].astype(F32) for p, first in parts)
                partial_out[h, at] = total
                weighted_out[h, at] = total * wide(gains_ref, row, width, tokens)


def branch_kernel(features, weighted_ref, inputs_ref, *refs):
    sums, (branch_out, other_out, upside_out) = refs[:-3], refs[-3:]
    _, part, tokens = branch_out.shape
    width = tile_of(part)
    both = jnp.sum(sum(s[...] for s in sums).reshape(2, 8, tokens), axis=1)
    upside = lax.rsqrt(both[:1] / features + epsilon)
    factor = both[1:] * (upside * upside * upside / features)
    upside_out[...] = jnp.broadcast_to(upside, upside_out.shape)
    for start in range(0, 2 * part, width):
        h, at = start // part, pl.ds(start % part, width)
        value = inputs_ref[pl.ds(start, width)].astype(F32)
        branch_out[h, at] = weighted_ref[h, at] * upside - value * factor
    core = lax.axis_index("section") & 1
    other_out[...] = branch_out[1 - core].astype(other_out.dtype)


def chip_of(distance):
    return (lax.axis_index("section") >> 1) ^ distance


def order_of(chips):
    return sorted(range(chips), key=lambda k: (k % 2 == 0, -k))


def pair_kernel(branch_ref, came_ref, *outs):
    core = lax.axis_index("section") & 1
    for k, out in enumerate(outs):
        q = chip_of(k)
        out[...] = (branch_ref[core, q] + came_ref[q].astype(F32)).astype(out.dtype)


def gain_grad_kernel(partial_ref, inputs_ref, upside_ref, out_ref, done_ref):
    done_ref[...] = upside_ref[...]
    _, part, tokens = partial_ref.shape
    width = tile_of(part)
    for start in range(0, 2 * part, width):
        product = partial_ref[start // part, pl.ds(start % part, width)] * upside_ref[:1]
        product = product * inputs_ref[pl.ds(start, width)].astype(F32)
        out_ref[:, start : start + width] = jnp.sum(product.T, axis=0, keepdims=True)


def later_kernel(*refs):
    chips = len(refs) // 2 - 1
    held, order = refs[-1], order_of(chips)
    for k in range(chips):
        held[chip_of(k)] = refs[order.index(k)][...].astype(F32)
    total = jnp.zeros(held.shape[1:], F32)
    for z in range(chips - 1, -1, -1):
        term = held[z]
        held[z] = total
        total = total + term
    for k in range(chips):
        out = refs[chips + 1 + k]
        out[...] = held[chip_of(k)].astype(out.dtype)


def mate_kernel(branch_ref, *refs):
    later, (later_out, mate_out) = refs[:-2], refs[-2:]
    core = lax.axis_index("section") & 1
    scale = core.astype(F32)
    for k, part in zip(order_of(len(later)), later):
        q = chip_of(k)
        later_out[q] = part[...]
        mate_out[q] = (part[...].astype(F32) + branch_ref[core, q] * scale).astype(mate_out.dtype)


def first_end_kernel(branch_ref, top_ref, later_ref, came_ref, out_ref):
    core = lax.axis_index("section") & 1
    pair = came_ref[...].astype(F32) * (1 - core).astype(F32)
    total = branch_ref[core] + top_ref[core].astype(F32) + later_ref[...].astype(F32) + pair
    out_ref[0] = total.astype(out_ref.dtype)


def second_end_kernel(branch_ref, top_ref, mate_ref, result_ref, out_ref):
    del result_ref
    other = 1 - (lax.axis_index("section") & 1)
    total = branch_ref[other] + top_ref[other].astype(F32) + mate_ref[...].astype(F32)
    out_ref[0] = total.astype(out_ref.dtype)


def call(kernel, out_shape, *arrays, cost=None):
    return pl.pallas_call(
        kernel,
        out_shape=out_shape,
        in_specs=[WHOLE] * len(arrays),
        out_specs=jax.tree.map(lambda _: WHOLE, out_shape),
        compiler_params=LIMIT,
        cost_estimate=cost,
    )(*(near(a) for a in arrays))


def local(features, layer_inputs, norm_gains, projection, head_grads, top_grads):
    count = lax.axis_size("tensor")
    layers = lax.axis_size("section")
    chips = layers // 2
    weight = projection[0]
    grads = head_grads[0]
    inputs = layer_inputs[0]
    rows, tokens = inputs.shape
    part = rows // 2
    sub = part // chips
    steps = count.bit_length() - 1

    def exchange(value, mask):
        return lax.ppermute(value, "tensor", [(i, i ^ mask) for i in range(count)])

    def swap(value):
        return lax.ppermute(value, "section", [(s, s ^ 1) for s in range(layers)])

    def across(value, distance):
        if not distance:
            return value
        return lax.ppermute(value, "section", [(s, s ^ (2 * distance)) for s in range(layers)])

    units = count // 2
    sent = [product(units, weight, grads, count, (), PIECES, a) for a in range(PIECES)]
    held = [[exchange(sent[a][h], mask_of(h, 0, count)) for h in range(2)] for a in range(PIECES)]
    *kept, squares = product(0, weight, grads, count, (inputs,))

    size = part // PIECES
    for step in range(1, steps):
        units //= 2
        for a in range(PIECES):
            last = step == steps - 1 and a == 0
            outs = [pltpu.VMEM((units + last, size, tokens), BF16)] * 2
            if last:
                kernel = lambda *refs: last_add_kernel(PIECES, *refs)
                total = call(kernel, outs, inputs, norm_gains, *kept, *held[a])
            else:
                total = call(lambda *refs: add_kernel(a, PIECES, *refs), outs, *kept, *held[a])
            held[a] = held[a] + [exchange(total[h], mask_of(h, step, count)) for h in range(2)]
    arrived = [v for step in range(steps) for a in range(PIECES) for v in held[a][2 * step : 2 * step + 2]]
    done = 2 * PIECES * (steps - 1)
    early = call(
        lambda *refs: early_kernel(PIECES, *refs),
        [
            pltpu.VMEM((8, tokens), F32),
            pltpu.VMEM((2, size, tokens), F32),
            pltpu.VMEM((2, part - size, tokens), F32),
        ],
        *kept,
        *arrived[:done],
        inputs,
        norm_gains,
        cost=pl.CostEstimate(flops=1 << 32, bytes_accessed=1 << 20, transcendentals=0),
    )
    sums = call(
        lambda *refs: inner_kernel(PIECES, *refs),
        pltpu.VMEM((16, tokens), F32),
        *early,
        squares,
        *arrived[done:-2],
    )
    sums, low = [sums], 1
    while low < count:
        group = [low] if 2 * low >= count else [2 * low, 1 * low, 3 * low]
        total = sum(sums)
        sums = [total] + [exchange(total, m) for m in group]
        low *= 4

    half = pltpu.VMEM((part, tokens), BF16)
    full = pltpu.VMEM((2, part, tokens), F32)
    held = [*kept, *arrived]
    partial_value, weighted = call(
        lambda *refs: weigh_kernel(PIECES, len(held), *refs),
        [full, full],
        *held,
        norm_gains,
        cost=pl.CostEstimate(flops=1 << 32, bytes_accessed=1 << 20, transcendentals=0),
    )
    branch, other, upside = call(
        lambda *refs: branch_kernel(features, *refs),
        [full, half, pltpu.VMEM((8, tokens), F32)],
        weighted,
        inputs,
        *sums,
    )

    shape = (chips, sub, tokens)
    block, whole = pltpu.VMEM((sub, tokens), BF16), pltpu.VMEM(shape, BF16)
    pair = swap(other)
    halves = branch.reshape(2, *shape)
    terms = call(pair_kernel, [block] * chips, halves, pair.reshape(shape))
    terms = [across(v, k) for k, v in enumerate(terms)]
    gain_grad, done = call(
        gain_grad_kernel,
        [jax.ShapeDtypeStruct((1, rows), F32), pltpu.VMEM((8, tokens), F32)],
        partial_value,
        inputs,
        upside,
    )
    later = pl.pallas_call(
        later_kernel,
        out_shape=[block] * chips,
        in_specs=[WHOLE] * chips + [pl.BlockSpec(memory_space=pl.ANY)],
        out_specs=[WHOLE] * chips,
        scratch_shapes=[pltpu.VMEM(shape, F32)],
        compiler_params=LIMIT,
    )(*(near(terms[k]) for k in order_of(chips)), done)
    later = [across(v, k) for k, v in enumerate(later)]
    later, mate = call(mate_kernel, [whole] * 2, halves, *(later[k] for k in order_of(chips)))
    later, mate = later.reshape(part, tokens), swap(mate.reshape(part, tokens))
    top = near(top_grads.reshape(2, part, tokens))

    def end(kernel, half, arrays, into):
        return pl.pallas_call(
            kernel,
            out_shape=jax.ShapeDtypeStruct((2, part, tokens), BF16),
            grid=(1,),
            in_specs=[WHOLE] * len(arrays) + [pl.BlockSpec(memory_space=pl.ANY)] * len(into),
            out_specs=pl.BlockSpec((1, part, tokens), lambda i: (half(lax.axis_index("section") & 1), 0, 0)),
            input_output_aliases={len(arrays): 0} if into else {},
            compiler_params=LIMIT,
        )(*(near(a) for a in arrays), *into)

    result = end(first_end_kernel, lambda core: core, (branch, top, later, pair), ())
    result = end(second_end_kernel, lambda core: 1 - core, (branch, top, mate), (result,))
    return (result.reshape(1, rows, tokens), gain_grad)


def solution(mesh):
    placed = (
        P("section", "tensor", None),
        P("section", "tensor"),
        P("section", None, "tensor"),
        P("section", None, "tensor"),
        P("tensor", None),
    )

    def whole(layer_inputs, norm_gains, projection, head_grads, top_grads):
        def part(*arrays):
            return local(layer_inputs.shape[1], *arrays)

        return jax.shard_map(
            part,
            mesh=mesh,
            in_specs=placed,
            out_specs=(P("section", "tensor", None), P("section", "tensor")),
            check_vma=False,
        )(layer_inputs, norm_gains, projection, head_grads, top_grads)

    return whole
```

```python
import jax
import jax.numpy as jnp
from jax import lax
from jax.experimental import pallas as pl
from jax.experimental.pallas import tpu as pltpu
from jax.sharding import PartitionSpec as P

epsilon = 1e-05
F32 = jnp.float32
BF16 = jnp.bfloat16
PIECES = 2
WHOLE = pl.BlockSpec(memory_space=pltpu.VMEM)
LIMIT = pltpu.CompilerParams(vmem_limit_bytes=16 << 20)


def near(value):
    return pltpu.with_memory_space_constraint(value, pltpu.VMEM)


def far(value):
    return pltpu.with_memory_space_constraint(value, pltpu.HBM)


def block_of(stream, j, count):
    bits = count.bit_length() - 1
    if stream == 1:
        return j
    out = 0
    for b in range(bits):
        out = out | (((j >> b) & 1) << (bits - 1 - b))
    return out


def mask_of(stream, step, count):
    return 1 << step if stream == 0 else count >> (step + 1)


def multiply(first_ref, second_ref, grads_ref, first_out, second_out):
    for weight, out in ((first_ref, first_out), (second_ref, second_out)):
        out[0] = lax.dot_general(
            weight[...], grads_ref[...], (((1,), (1,)), ((), ())), preferred_element_type=F32
        ).astype(out.dtype)


def tile_of(part):
    return min(part, 128)


def wide(gains_ref, start, width, tokens):
    return jnp.broadcast_to(gains_ref[:, start : start + width], (tokens, width)).T


def keep_kernel(first_ref, second_ref, grads_ref, inputs_ref, first_out, second_out, squares_out):
    rows, tokens = inputs_ref.shape
    width = tile_of(rows)

    @pl.when(pl.program_id(0) == 0)
    def _():
        total = jnp.zeros((8, tokens), F32)
        for start in range(0, rows, width):
            value = inputs_ref[pl.ds(start, width)].astype(F32)
            total = total + jnp.sum((value * value).reshape(width // 8, 8, tokens), axis=0)
        squares_out[...] = total

    multiply(first_ref, second_ref, grads_ref, first_out, second_out)


def product(base, weight, grads, count, extra=(), pieces=1, piece=0):
    features, depth = weight.shape
    tokens = grads.shape[0]
    part = features // count // 2 // pieces
    units = count // 2

    def rows_of(stream):
        def at(i):
            block = lax.axis_index("tensor") ^ block_of(stream, i + base, count)
            return ((block * 2 + stream) * pieces + piece, 0)

        return at

    out = pltpu.VMEM((units, part, tokens), BF16)
    out_shape, out_specs = [out, out], [pl.BlockSpec((1, part, tokens), lambda i: (i, 0, 0))] * 2
    if extra:
        out_shape.append(pltpu.VMEM((8, tokens), F32))
        out_specs.append(WHOLE)
    return pl.pallas_call(
        keep_kernel if extra else multiply,
        out_shape=out_shape,
        grid=(units,),
        in_specs=[
            pl.BlockSpec((part, depth), rows_of(0)),
            pl.BlockSpec((part, depth), rows_of(1)),
            pl.BlockSpec((tokens, depth), lambda i: (0, 0)),
        ]
        + [WHOLE] * len(extra),
        out_specs=out_specs,
        compiler_params=LIMIT,
        cost_estimate=pl.CostEstimate(
            flops=4 * units * part * depth * tokens,
            bytes_accessed=4 * units * part * (depth + tokens),
            transcendentals=0,
        ),
    )(far(weight), far(weight), far(grads), *extra)


def terms_of(refs, pieces, stream, piece):
    kept, came = refs[stream], refs[2 + 2 * piece + stream :: 2 * pieces]
    return [(kept, piece * (kept.shape[1] // pieces))] + [(c, 0) for c in came]


def add_kernel(piece, pieces, *refs):
    outs = refs[-2:]
    for h, out in enumerate(outs):
        units, size, _ = out.shape
        width = tile_of(size)
        kept = refs[h]
        parts = [(kept, piece * size)] + [(c, 0) for c in refs[2 + h : -2 : 2]]
        for u in range(units):
            for start in range(0, size, width):
                total = sum(p[u + units, pl.ds(first + start, width)].astype(F32) for p, first in parts)
                out[u, pl.ds(start, width)] = total.astype(out.dtype)


def last_add_kernel(pieces, inputs_ref, gains_ref, *refs):
    add_kernel(0, pieces, *refs[:-2], *(out.at[:1] for out in refs[-2:]))
    rows, tokens = inputs_ref.shape
    part = rows // 2
    for h, out in enumerate(refs[-2:]):
        size = out.shape[1]
        width = tile_of(size)
        for start in range(0, size, width):
            row = (h + 1) * part - size + start
            gained = inputs_ref[pl.ds(row, width)].astype(F32) * wide(gains_ref, row, width, tokens)
            out[1, pl.ds(start, width)] = gained.astype(out.dtype)


def early_kernel(pieces, *refs):
    held, (inputs_ref, gains_ref, inner_out, pairs_out, gained_out) = refs[:-5], refs[-5:]
    part = held[0].shape[1]
    tokens = inputs_ref.shape[1]
    size = part // pieces
    width = tile_of(size)
    inner = jnp.zeros((8, tokens), F32)
    for h in range(2):
        for a in range(pieces):
            parts = terms_of(held, pieces, h, a)
            for start in range(0, size, width):
                row = h * part + a * size + start
                factor = wide(gains_ref, row, width, tokens) * inputs_ref[pl.ds(row, width)].astype(F32)
                product = sum(p[0, pl.ds(first + start, width)].astype(F32) for p, first in parts) * factor
                inner = inner + jnp.sum(product.reshape(width // 8, 8, tokens), axis=0)
                if a == pieces - 1:
                    total = sum(p[1, pl.ds(first + start, width)].astype(F32) for p, first in parts)
                    pairs_out[h, pl.ds(start, width)] = total
                else:
                    gained_out[h, pl.ds(a * size + start, width)] = factor
    inner_out[...] = inner


def inner_kernel(pieces, inner_ref, pairs_ref, gained_ref, squares_ref, *refs):
    came, sums_out = refs[:-1], refs[-1]
    _, size, tokens = pairs_ref.shape
    width = tile_of(size)
    inner = inner_ref[...]
    for h in range(2):
        for start in range(0, size, width):
            at = pl.ds(start, width)
            product = pairs_ref[h, at] * came[h][1, at].astype(F32)
            for a in range(pieces - 1):
                product = product + gained_ref[h, pl.ds(a * size + start, width)] * came[2 * a + h][0, at].astype(F32)
            inner = inner + jnp.sum(product.reshape(width // 8, 8, tokens), axis=0)
    sums_out[...] = jnp.concatenate([squares_ref[...], inner])


def weigh_kernel(pieces, held, *refs):
    blocks, (gains_ref, partial_out, weighted_out) = refs[:held], refs[held:]
    part, tokens = partial_out.shape[1:]
    size = part // pieces
    width = tile_of(size)
    for h in range(2):
        for a in range(pieces):
            parts = terms_of(blocks, pieces, h, a)
            for start in range(0, size, width):
                at = pl.ds(a * size + start, width)
                row = h * part + a * size + start
                total = sum(p[0, pl.ds(first + start, width)].astype(F32) for p, first in parts)
                partial_out[h, at] = total
                weighted_out[h, at] = total * wide(gains_ref, row, width, tokens)


def branch_kernel(features, weighted_ref, inputs_ref, *refs):
    sums, (branch_out, other_out, upside_out) = refs[:-3], refs[-3:]
    _, part, tokens = branch_out.shape
    width = tile_of(part)
    both = jnp.sum(sum(s[...] for s in sums).reshape(2, 8, tokens), axis=1)
    upside = lax.rsqrt(both[:1] / features + epsilon)
    factor = both[1:] * (upside * upside * upside / features)
    upside_out[...] = jnp.broadcast_to(upside, upside_out.shape)
    for start in range(0, 2 * part, width):
        h, at = start // part, pl.ds(start % part, width)
        value = inputs_ref[pl.ds(start, width)].astype(F32)
        branch_out[h, at] = weighted_ref[h, at] * upside - value * factor
    core = lax.axis_index("section") & 1
    other_out[...] = branch_out[1 - core].astype(other_out.dtype)


def chip_of(distance):
    return (lax.axis_index("section") >> 1) ^ distance


def order_of(chips):
    return sorted(range(chips), key=lambda k: (k % 2 == 0, -k))


def pair_kernel(branch_ref, came_ref, *outs):
    core = lax.axis_index("section") & 1
    for k, out in enumerate(outs):
        q = chip_of(k)
        out[...] = (branch_ref[core, q] + came_ref[q].astype(F32)).astype(out.dtype)


def gain_grad_kernel(partial_ref, inputs_ref, upside_ref, out_ref, done_ref):
    done_ref[...] = upside_ref[...]
    _, part, tokens = partial_ref.shape
    width = tile_of(part)
    for start in range(0, 2 * part, width):
        product = partial_ref[start // part, pl.ds(start % part, width)] * upside_ref[:1]
        product = product * inputs_ref[pl.ds(start, width)].astype(F32)
        out_ref[:, start : start + width] = jnp.sum(product.T, axis=0, keepdims=True)


def later_kernel(*refs):
    chips = len(refs) // 2 - 1
    held, order = refs[-1], order_of(chips)
    for k in range(chips):
        held[chip_of(k)] = refs[order.index(k)][...].astype(F32)
    total = jnp.zeros(held.shape[1:], F32)
    for z in range(chips - 1, -1, -1):
        term = held[z]
        held[z] = total
        total = total + term
    for k in range(chips):
        out = refs[chips + 1 + k]
        out[...] = held[chip_of(k)].astype(out.dtype)


def mate_kernel(branch_ref, top_ref, came_ref, *refs):
    later, (later_out, mate_out) = refs[:-2], refs[-2:]
    core = lax.axis_index("section") & 1
    scale = core.astype(F32)
    for k, part in zip(order_of(len(later)), later):
        q = chip_of(k)
        later_out[q] = part[...]
        rest = top_ref[core, q].astype(F32) + came_ref[q].astype(F32) + branch_ref[core, q] * scale
        mate_out[q] = (part[...].astype(F32) + rest).astype(mate_out.dtype)


def first_end_kernel(branch_ref, top_ref, later_ref, came_ref, out_ref):
    core = lax.axis_index("section") & 1
    pair = came_ref[...].astype(F32) * (1 - core).astype(F32)
    total = branch_ref[core] + top_ref[core].astype(F32) + later_ref[...].astype(F32) + pair
    out_ref[0] = total.astype(out_ref.dtype)


def second_end_kernel(mate_ref, result_ref, out_ref, done):
    del result_ref
    other = 1 - (lax.axis_index("section") & 1)
    copy = pltpu.make_async_copy(mate_ref, out_ref.at[other], done)
    copy.start()
    copy.wait()


def call(kernel, out_shape, *arrays, cost=None):
    return pl.pallas_call(
        kernel,
        out_shape=out_shape,
        in_specs=[WHOLE] * len(arrays),
        out_specs=jax.tree.map(lambda _: WHOLE, out_shape),
        compiler_params=LIMIT,
        cost_estimate=cost,
    )(*(near(a) for a in arrays))


def local(features, layer_inputs, norm_gains, projection, head_grads, top_grads):
    count = lax.axis_size("tensor")
    layers = lax.axis_size("section")
    chips = layers // 2
    weight = projection[0]
    grads = head_grads[0]
    inputs = layer_inputs[0]
    rows, tokens = inputs.shape
    part = rows // 2
    sub = part // chips
    steps = count.bit_length() - 1

    def exchange(value, mask):
        return lax.ppermute(value, "tensor", [(i, i ^ mask) for i in range(count)])

    def swap(value):
        return lax.ppermute(value, "section", [(s, s ^ 1) for s in range(layers)])

    def across(value, distance):
        if not distance:
            return value
        return lax.ppermute(value, "section", [(s, s ^ (2 * distance)) for s in range(layers)])

    units = count // 2
    sent = [product(units, weight, grads, count, (), PIECES, a) for a in range(PIECES)]
    held = [[exchange(sent[a][h], mask_of(h, 0, count)) for h in range(2)] for a in range(PIECES)]
    *kept, squares = product(0, weight, grads, count, (inputs,))

    size = part // PIECES
    for step in range(1, steps):
        units //= 2
        for a in range(PIECES):
            last = step == steps - 1 and a == 0
            outs = [pltpu.VMEM((units + last, size, tokens), BF16)] * 2
            if last:
                kernel = lambda *refs: last_add_kernel(PIECES, *refs)
                total = call(kernel, outs, inputs, norm_gains, *kept, *held[a])
            else:
                total = call(lambda *refs: add_kernel(a, PIECES, *refs), outs, *kept, *held[a])
            held[a] = held[a] + [exchange(total[h], mask_of(h, step, count)) for h in range(2)]
    arrived = [v for step in range(steps) for a in range(PIECES) for v in held[a][2 * step : 2 * step + 2]]
    done = 2 * PIECES * (steps - 1)
    early = call(
        lambda *refs: early_kernel(PIECES, *refs),
        [
            pltpu.VMEM((8, tokens), F32),
            pltpu.VMEM((2, size, tokens), F32),
            pltpu.VMEM((2, part - size, tokens), F32),
        ],
        *kept,
        *arrived[:done],
        inputs,
        norm_gains,
        cost=pl.CostEstimate(flops=1 << 32, bytes_accessed=1 << 20, transcendentals=0),
    )
    sums = call(
        lambda *refs: inner_kernel(PIECES, *refs),
        pltpu.VMEM((16, tokens), F32),
        *early,
        squares,
        *arrived[done:-2],
    )
    sums, low = [sums], 1
    while low < count:
        group = [low] if 2 * low >= count else [2 * low, 1 * low, 3 * low]
        total = sum(sums)
        sums = [total] + [exchange(total, m) for m in group]
        low *= 4

    half = pltpu.VMEM((part, tokens), BF16)
    full = pltpu.VMEM((2, part, tokens), F32)
    held = [*kept, *arrived]
    partial_value, weighted = call(
        lambda *refs: weigh_kernel(PIECES, len(held), *refs),
        [full, full],
        *held,
        norm_gains,
        cost=pl.CostEstimate(flops=1 << 32, bytes_accessed=1 << 20, transcendentals=0),
    )
    branch, other, upside = call(
        lambda *refs: branch_kernel(features, *refs),
        [full, half, pltpu.VMEM((8, tokens), F32)],
        weighted,
        inputs,
        *sums,
    )

    shape = (chips, sub, tokens)
    block, whole = pltpu.VMEM((sub, tokens), BF16), pltpu.VMEM(shape, BF16)
    pair = swap(other)
    halves = branch.reshape(2, *shape)
    terms = call(pair_kernel, [block] * chips, halves, pair.reshape(shape))
    terms = [across(v, k) for k, v in enumerate(terms)]
    gain_grad, done = call(
        gain_grad_kernel,
        [jax.ShapeDtypeStruct((1, rows), F32), pltpu.VMEM((8, tokens), F32)],
        partial_value,
        inputs,
        upside,
    )
    later = pl.pallas_call(
        later_kernel,
        out_shape=[block] * chips,
        in_specs=[WHOLE] * chips + [pl.BlockSpec(memory_space=pl.ANY)],
        out_specs=[WHOLE] * chips,
        scratch_shapes=[pltpu.VMEM(shape, F32)],
        compiler_params=LIMIT,
    )(*(near(terms[k]) for k in order_of(chips)), done)
    later = [across(v, k) for k, v in enumerate(later)]
    top = top_grads.reshape(2, part, tokens)
    later, mate = call(
        mate_kernel,
        [whole] * 2,
        halves,
        top.reshape(2, *shape),
        pair.reshape(shape),
        *(later[k] for k in order_of(chips)),
    )
    later, mate = later.reshape(part, tokens), swap(mate.reshape(part, tokens))
    arrays = (branch, top, later, pair)
    result = pl.pallas_call(
        first_end_kernel,
        out_shape=jax.ShapeDtypeStruct((2, part, tokens), BF16),
        grid=(1,),
        in_specs=[WHOLE] * len(arrays),
        out_specs=pl.BlockSpec((1, part, tokens), lambda i: (lax.axis_index("section") & 1, 0, 0)),
        compiler_params=LIMIT,
    )(*(near(a) for a in arrays))
    result = pl.pallas_call(
        second_end_kernel,
        out_shape=jax.ShapeDtypeStruct((2, part, tokens), BF16),
        in_specs=[WHOLE, pl.BlockSpec(memory_space=pl.ANY)],
        out_specs=pl.BlockSpec(memory_space=pl.ANY),
        scratch_shapes=[pltpu.SemaphoreType.DMA],
        input_output_aliases={1: 0},
        compiler_params=LIMIT,
    )(near(mate), result)
    return (result.reshape(1, rows, tokens), gain_grad)


def solution(mesh):
    placed = (
        P("section", "tensor", None),
        P("section", "tensor"),
        P("section", None, "tensor"),
        P("section", None, "tensor"),
        P("tensor", None),
    )

    def whole(layer_inputs, norm_gains, projection, head_grads, top_grads):
        def part(*arrays):
            return local(layer_inputs.shape[1], *arrays)

        return jax.shard_map(
            part,
            mesh=mesh,
            in_specs=placed,
            out_specs=(P("section", "tensor", None), P("section", "tensor")),
            check_vma=False,
        )(layer_inputs, norm_gains, projection, head_grads, top_grads)

    return whole
```

```python
import jax
import jax.numpy as jnp
from jax import lax
from jax.experimental import pallas as pl
from jax.experimental.pallas import tpu as pltpu
from jax.sharding import PartitionSpec as P

epsilon = 1e-05
F32 = jnp.float32
BF16 = jnp.bfloat16
PIECES = 2
WHOLE = pl.BlockSpec(memory_space=pltpu.VMEM)
LIMIT = pltpu.CompilerParams(vmem_limit_bytes=16 << 20)


def near(value):
    return pltpu.with_memory_space_constraint(value, pltpu.VMEM)


def far(value):
    return pltpu.with_memory_space_constraint(value, pltpu.HBM)


def block_of(stream, j, count):
    bits = count.bit_length() - 1
    if stream == 1:
        return j
    out = 0
    for b in range(bits):
        out = out | (((j >> b) & 1) << (bits - 1 - b))
    return out


def mask_of(stream, step, count):
    return 1 << step if stream == 0 else count >> (step + 1)


def multiply(first_ref, second_ref, grads_ref, first_out, second_out):
    for weight, out in ((first_ref, first_out), (second_ref, second_out)):
        out[0] = lax.dot_general(
            weight[...], grads_ref[...], (((1,), (1,)), ((), ())), preferred_element_type=F32
        ).astype(out.dtype)


def tile_of(part):
    return min(part, 128)


def wide(gains_ref, start, width, tokens):
    return jnp.broadcast_to(gains_ref[:, start : start + width], (tokens, width)).T


def keep_kernel(first_ref, second_ref, grads_ref, inputs_ref, first_out, second_out, squares_out):
    rows, tokens = inputs_ref.shape
    width = tile_of(rows)

    @pl.when(pl.program_id(0) == 0)
    def _():
        total = jnp.zeros((8, tokens), F32)
        for start in range(0, rows, width):
            value = inputs_ref[pl.ds(start, width)].astype(F32)
            total = total + jnp.sum((value * value).reshape(width // 8, 8, tokens), axis=0)
        squares_out[...] = total

    multiply(first_ref, second_ref, grads_ref, first_out, second_out)


def product(base, weight, grads, count, extra=(), pieces=1, piece=0):
    features, depth = weight.shape
    tokens = grads.shape[0]
    part = features // count // 2 // pieces
    units = count // 2

    def rows_of(stream):
        def at(i):
            block = lax.axis_index("tensor") ^ block_of(stream, i + base, count)
            return ((block * 2 + stream) * pieces + piece, 0)

        return at

    out = pltpu.VMEM((units, part, tokens), BF16)
    out_shape, out_specs = [out, out], [pl.BlockSpec((1, part, tokens), lambda i: (i, 0, 0))] * 2
    if extra:
        out_shape.append(pltpu.VMEM((8, tokens), F32))
        out_specs.append(WHOLE)
    return pl.pallas_call(
        keep_kernel if extra else multiply,
        out_shape=out_shape,
        grid=(units,),
        in_specs=[
            pl.BlockSpec((part, depth), rows_of(0)),
            pl.BlockSpec((part, depth), rows_of(1)),
            pl.BlockSpec((tokens, depth), lambda i: (0, 0)),
        ]
        + [WHOLE] * len(extra),
        out_specs=out_specs,
        compiler_params=LIMIT,
        cost_estimate=pl.CostEstimate(
            flops=4 * units * part * depth * tokens,
            bytes_accessed=4 * units * part * (depth + tokens),
            transcendentals=0,
        ),
    )(far(weight), far(weight), far(grads), *extra)


def terms_of(refs, pieces, stream, piece):
    kept, came = refs[stream], refs[2 + 2 * piece + stream :: 2 * pieces]
    return [(kept, piece * (kept.shape[1] // pieces))] + [(c, 0) for c in came]


def add_kernel(piece, pieces, *refs):
    outs = refs[-2:]
    for h, out in enumerate(outs):
        units, size, _ = out.shape
        width = tile_of(size)
        kept = refs[h]
        parts = [(kept, piece * size)] + [(c, 0) for c in refs[2 + h : -2 : 2]]
        for u in range(units):
            for start in range(0, size, width):
                total = sum(p[u + units, pl.ds(first + start, width)].astype(F32) for p, first in parts)
                out[u, pl.ds(start, width)] = total.astype(out.dtype)


def last_add_kernel(pieces, inputs_ref, gains_ref, *refs):
    add_kernel(0, pieces, *refs[:-2], *(out.at[:1] for out in refs[-2:]))
    rows, tokens = inputs_ref.shape
    part = rows // 2
    for h, out in enumerate(refs[-2:]):
        size = out.shape[1]
        width = tile_of(size)
        for start in range(0, size, width):
            row = (h + 1) * part - size + start
            gained = inputs_ref[pl.ds(row, width)].astype(F32) * wide(gains_ref, row, width, tokens)
            out[1, pl.ds(start, width)] = gained.astype(out.dtype)


def early_kernel(pieces, *refs):
    held, (inputs_ref, gains_ref, inner_out, pairs_out, gained_out) = refs[:-5], refs[-5:]
    part = held[0].shape[1]
    tokens = inputs_ref.shape[1]
    size = part // pieces
    width = tile_of(size)
    inner = jnp.zeros((8, tokens), F32)
    for h in range(2):
        for a in range(pieces):
            parts = terms_of(held, pieces, h, a)
            for start in range(0, size, width):
                row = h * part + a * size + start
                factor = wide(gains_ref, row, width, tokens) * inputs_ref[pl.ds(row, width)].astype(F32)
                product = sum(p[0, pl.ds(first + start, width)].astype(F32) for p, first in parts) * factor
                inner = inner + jnp.sum(product.reshape(width // 8, 8, tokens), axis=0)
                if a == pieces - 1:
                    total = sum(p[1, pl.ds(first + start, width)].astype(F32) for p, first in parts)
                    pairs_out[h, pl.ds(start, width)] = total
                else:
                    gained_out[h, pl.ds(a * size + start, width)] = factor
    inner_out[...] = inner


def inner_kernel(pieces, inner_ref, pairs_ref, gained_ref, squares_ref, *refs):
    came, sums_out = refs[:-1], refs[-1]
    _, size, tokens = pairs_ref.shape
    width = tile_of(size)
    inner = inner_ref[...]
    for h in range(2):
        for start in range(0, size, width):
            at = pl.ds(start, width)
            product = pairs_ref[h, at] * came[h][1, at].astype(F32)
            for a in range(pieces - 1):
                product = product + gained_ref[h, pl.ds(a * size + start, width)] * came[2 * a + h][0, at].astype(F32)
            inner = inner + jnp.sum(product.reshape(width // 8, 8, tokens), axis=0)
    sums_out[...] = jnp.concatenate([squares_ref[...], inner])


def weigh_kernel(pieces, held, *refs):
    blocks, (gains_ref, partial_out, weighted_out) = refs[:held], refs[held:]
    part, tokens = partial_out.shape[1:]
    size = part // pieces
    width = tile_of(size)
    for h in range(2):
        for a in range(pieces):
            parts = terms_of(blocks, pieces, h, a)
            for start in range(0, size, width):
                at = pl.ds(a * size + start, width)
                row = h * part + a * size + start
                total = sum(p[0, pl.ds(first + start, width)].astype(F32) for p, first in parts)
                partial_out[h, at] = total
                weighted_out[h, at] = total * wide(gains_ref, row, width, tokens)


def branch_kernel(features, weighted_ref, inputs_ref, *refs):
    sums, (branch_out, other_out, upside_out) = refs[:-3], refs[-3:]
    _, part, tokens = branch_out.shape
    width = tile_of(part)
    both = jnp.sum(sum(s[...] for s in sums).reshape(2, 8, tokens), axis=1)
    upside = lax.rsqrt(both[:1] / features + epsilon)
    factor = both[1:] * (upside * upside * upside / features)
    upside_out[...] = jnp.broadcast_to(upside, upside_out.shape)
    for start in range(0, 2 * part, width):
        h, at = start // part, pl.ds(start % part, width)
        value = inputs_ref[pl.ds(start, width)].astype(F32)
        branch_out[h, at] = weighted_ref[h, at] * upside - value * factor
    core = lax.axis_index("section") & 1
    other_out[...] = branch_out[1 - core].astype(other_out.dtype)


def chip_of(distance):
    return (lax.axis_index("section") >> 1) ^ distance


def order_of(chips):
    return sorted(range(chips), key=lambda k: (k % 2 == 0, -k))


def pair_kernel(branch_ref, came_ref, *outs):
    core = lax.axis_index("section") & 1
    for k, out in enumerate(outs):
        q = chip_of(k)
        out[...] = (branch_ref[core, q] + came_ref[q].astype(F32)).astype(out.dtype)


def gain_grad_kernel(partial_ref, inputs_ref, upside_ref, out_ref, done_ref):
    done_ref[...] = upside_ref[...]
    _, part, tokens = partial_ref.shape
    width = tile_of(part)
    for start in range(0, 2 * part, width):
        product = partial_ref[start // part, pl.ds(start % part, width)] * upside_ref[:1]
        product = product * inputs_ref[pl.ds(start, width)].astype(F32)
        out_ref[:, start : start + width] = jnp.sum(product.T, axis=0, keepdims=True)


def later_kernel(*refs):
    chips = len(refs) // 2 - 1
    held, order = refs[-1], order_of(chips)
    for k in range(chips):
        held[chip_of(k)] = refs[order.index(k)][...].astype(F32)
    total = jnp.zeros(held.shape[1:], F32)
    for z in range(chips - 1, -1, -1):
        term = held[z]
        held[z] = total
        total = total + term
    for k in range(chips):
        out = refs[chips + 1 + k]
        out[...] = held[chip_of(k)].astype(out.dtype)


def mate_kernel(branch_ref, top_ref, came_ref, *refs):
    later, (mine_out, mate_out) = refs[:-2], refs[-2:]
    core = lax.axis_index("section") & 1
    scale = core.astype(F32)
    for k, part in zip(order_of(len(later)), later):
        q = chip_of(k)
        base = top_ref[core, q].astype(F32) + part[...].astype(F32)
        came, own = came_ref[q].astype(F32), branch_ref[core, q]
        mine_out[q] = (base + own + came * (1 - scale)).astype(mine_out.dtype)
        mate_out[q] = (base + came + own * scale).astype(mate_out.dtype)


def end_kernel(mine_ref, mate_ref, out_ref, done):
    core = lax.axis_index("section") & 1
    copies = [
        pltpu.make_async_copy(mine_ref, out_ref.at[core], done.at[0]),
        pltpu.make_async_copy(mate_ref, out_ref.at[1 - core], done.at[1]),
    ]
    for copy in copies:
        copy.start()
    for copy in copies:
        copy.wait()


def call(kernel, out_shape, *arrays, cost=None):
    return pl.pallas_call(
        kernel,
        out_shape=out_shape,
        in_specs=[WHOLE] * len(arrays),
        out_specs=jax.tree.map(lambda _: WHOLE, out_shape),
        compiler_params=LIMIT,
        cost_estimate=cost,
    )(*(near(a) for a in arrays))


def local(features, layer_inputs, norm_gains, projection, head_grads, top_grads):
    count = lax.axis_size("tensor")
    layers = lax.axis_size("section")
    chips = layers // 2
    weight = projection[0]
    grads = head_grads[0]
    inputs = layer_inputs[0]
    rows, tokens = inputs.shape
    part = rows // 2
    sub = part // chips
    steps = count.bit_length() - 1

    def exchange(value, mask):
        return lax.ppermute(value, "tensor", [(i, i ^ mask) for i in range(count)])

    def swap(value):
        return lax.ppermute(value, "section", [(s, s ^ 1) for s in range(layers)])

    def across(value, distance):
        if not distance:
            return value
        return lax.ppermute(value, "section", [(s, s ^ (2 * distance)) for s in range(layers)])

    units = count // 2
    sent = [product(units, weight, grads, count, (), PIECES, a) for a in range(PIECES)]
    held = [[exchange(sent[a][h], mask_of(h, 0, count)) for h in range(2)] for a in range(PIECES)]
    *kept, squares = product(0, weight, grads, count, (inputs,))

    size = part // PIECES
    for step in range(1, steps):
        units //= 2
        for a in range(PIECES):
            last = step == steps - 1 and a == 0
            outs = [pltpu.VMEM((units + last, size, tokens), BF16)] * 2
            if last:
                kernel = lambda *refs: last_add_kernel(PIECES, *refs)
                total = call(kernel, outs, inputs, norm_gains, *kept, *held[a])
            else:
                total = call(lambda *refs: add_kernel(a, PIECES, *refs), outs, *kept, *held[a])
            held[a] = held[a] + [exchange(total[h], mask_of(h, step, count)) for h in range(2)]
    arrived = [v for step in range(steps) for a in range(PIECES) for v in held[a][2 * step : 2 * step + 2]]
    done = 2 * PIECES * (steps - 1)
    early = call(
        lambda *refs: early_kernel(PIECES, *refs),
        [
            pltpu.VMEM((8, tokens), F32),
            pltpu.VMEM((2, size, tokens), F32),
            pltpu.VMEM((2, part - size, tokens), F32),
        ],
        *kept,
        *arrived[:done],
        inputs,
        norm_gains,
        cost=pl.CostEstimate(flops=1 << 32, bytes_accessed=1 << 20, transcendentals=0),
    )
    sums = call(
        lambda *refs: inner_kernel(PIECES, *refs),
        pltpu.VMEM((16, tokens), F32),
        *early,
        squares,
        *arrived[done:-2],
    )
    sums, low = [sums], 1
    while low < count:
        group = [low] if 2 * low >= count else [2 * low, 1 * low, 3 * low]
        total = sum(sums)
        sums = [total] + [exchange(total, m) for m in group]
        low *= 4

    half = pltpu.VMEM((part, tokens), BF16)
    full = pltpu.VMEM((2, part, tokens), F32)
    held = [*kept, *arrived]
    partial_value, weighted = call(
        lambda *refs: weigh_kernel(PIECES, len(held), *refs),
        [full, full],
        *held,
        norm_gains,
        cost=pl.CostEstimate(flops=1 << 32, bytes_accessed=1 << 20, transcendentals=0),
    )
    branch, other, upside = call(
        lambda *refs: branch_kernel(features, *refs),
        [full, half, pltpu.VMEM((8, tokens), F32)],
        weighted,
        inputs,
        *sums,
    )

    shape = (chips, sub, tokens)
    block, whole = pltpu.VMEM((sub, tokens), BF16), pltpu.VMEM(shape, BF16)
    pair = swap(other)
    halves = branch.reshape(2, *shape)
    terms = call(pair_kernel, [block] * chips, halves, pair.reshape(shape))
    terms = [across(v, k) for k, v in enumerate(terms)]
    gain_grad, done = call(
        gain_grad_kernel,
        [jax.ShapeDtypeStruct((1, rows), F32), pltpu.VMEM((8, tokens), F32)],
        partial_value,
        inputs,
        upside,
    )
    later = pl.pallas_call(
        later_kernel,
        out_shape=[block] * chips,
        in_specs=[WHOLE] * chips + [pl.BlockSpec(memory_space=pl.ANY)],
        out_specs=[WHOLE] * chips,
        scratch_shapes=[pltpu.VMEM(shape, F32)],
        compiler_params=LIMIT,
    )(*(near(terms[k]) for k in order_of(chips)), done)
    later = [across(v, k) for k, v in enumerate(later)]
    top = top_grads.reshape(2, part, tokens)
    mine, mate = call(
        mate_kernel,
        [whole] * 2,
        halves,
        top.reshape(2, *shape),
        pair.reshape(shape),
        *(later[k] for k in order_of(chips)),
    )
    mine, mate = mine.reshape(part, tokens), swap(mate.reshape(part, tokens))
    result = pl.pallas_call(
        end_kernel,
        out_shape=jax.ShapeDtypeStruct((2, part, tokens), BF16),
        in_specs=[WHOLE] * 2,
        out_specs=pl.BlockSpec(memory_space=pl.ANY),
        scratch_shapes=[pltpu.SemaphoreType.DMA((2,))],
        compiler_params=LIMIT,
    )(near(mine), near(mate))
    return (result.reshape(1, rows, tokens), gain_grad)


def solution(mesh):
    placed = (
        P("section", "tensor", None),
        P("section", "tensor"),
        P("section", None, "tensor"),
        P("section", None, "tensor"),
        P("tensor", None),
    )

    def whole(layer_inputs, norm_gains, projection, head_grads, top_grads):
        def part(*arrays):
            return local(layer_inputs.shape[1], *arrays)

        return jax.shard_map(
            part,
            mesh=mesh,
            in_specs=placed,
            out_specs=(P("section", "tensor", None), P("section", "tensor")),
            check_vma=False,
        )(layer_inputs, norm_gains, projection, head_grads, top_grads)

    return whole
```
